256 devices in a mesh: wide: 32 (over z, y_lo, core), narrow: 8 (over y_hi, x).
Axes of the slice: x: 4, y: 4 (y_hi: 2, y_lo: 2; y = y_hi * 2 + y_lo), z: 8, core: 2. Of those that a mesh axis runs over, the one named last changes fastest.
Arguments:
- tokens: bfloat16 [3072, 8192], P('wide', 'narrow')
- grad_out: bfloat16 [3072, 8192], P('wide', 'narrow'), may hold values from -6 to 6
- selected: int32 [384], replicated, may hold values from 0 to 3071, as said below
- gain: float32 [8192], P('narrow'), may hold values from 0.1 to 1.9
- router_weight: float32 [8192], P('narrow'), may hold values from -0.0625 to 0.0625
- w_gate: bfloat16 [8192, 32768], P('narrow', 'wide'), may hold values from -0.0625 to 0.0625
- w_up: bfloat16 [8192, 32768], P('narrow', 'wide'), may hold values from -0.0625 to 0.0625
- w_down: bfloat16 [32768, 8192], P('wide', 'narrow'), may hold values from -0.03125 to 0.03125
Outputs:
- grad_x: bfloat16 [3072, 8192], P('wide', 'narrow')
- grad_gate: bfloat16 [8192, 32768], P('narrow', 'wide')
- grad_up: bfloat16 [8192, 32768], P('narrow', 'wide')
- grad_down: bfloat16 [32768, 8192], P('wide', 'narrow')
- grad_gain: float32 [8192], P('narrow')
- grad_router: float32 [8192], P('narrow')
The draws below stay inside these ranges and needn't reach their ends.
Inputs may be any that keep to these rules, and one draw needn't show every extreme that they name: The ids rise strictly. Each aligned block of 96 token ids holds at most 24 selected ids, and some block holds exactly 24.
All inputs are finite; a program needn't handle non-finite values.
Results may differ from the reference program's by a relative error of at most 0.008.
Values may be sent and summed in bfloat16 or wider, within the bound.
No kernel may reach another device: no remote copies, remote signals or barrier semaphores. Data moves between devices by JAX's collectives and lax.ppermute only.
A program may use at most 128 MiB of HBM per device.

```python
import math
import jax
import jax.numpy as jnp
from jax import lax

D = 8192
FF = 32768
TOK_DEV = 96
TOKENS = 3072
SEL = 384


def draw_selected(key, part):
    key = jax.random.fold_in(key, 11)
    blocks = TOKENS // TOK_DEV
    base = TOK_DEV // 8
    pairs = blocks // 2
    key_shift, key_pick, key_rank = jax.random.split(key, 3)
    shifts = jax.random.randint(key_shift, (pairs,), -base, base + 1)
    chosen = jax.random.randint(key_pick, (), 0, pairs)
    shifts = jnp.where(jnp.arange(pairs) == chosen, base, shifts)
    counts = jnp.stack([base + shifts, base - shifts], axis=1).reshape(blocks)
    ranks = jax.vmap(lambda k: jax.random.permutation(k, TOK_DEV))(jax.random.split(key_rank, blocks))
    marked = (ranks < counts[:, None]).reshape(TOKENS).astype(jnp.int32)
    order = jnp.argsort(1 - marked, stable=True)
    return order[:SEL].astype(jnp.int32)


def draw_tokens(key, part):
    key = jax.random.fold_in(key, 23)
    key_vals, key_rows = jax.random.split(key)
    values = jax.random.normal(key_vals, (TOKENS, D), jnp.float32)
    logs = jax.random.uniform(key_rows, (TOKENS, 1), jnp.float32, math.log(0.3), math.log(3.0))
    return (values * jnp.exp(logs)).astype(jnp.bfloat16)


def steps_of(own_key, extent, shards, least, top_value):
    def one(dim, shards_of):
        heights = jax.random.uniform(jax.random.fold_in(jax.random.fold_in(own_key, 6), dim), (shards_of,), jnp.float32, least / len(shards), top_value / len(shards))
        return jnp.repeat(jnp.exp(heights), extent[dim] // shards_of).reshape((-1,) + (1,) * (len(extent) - dim - 1))

    level = one(*shards[0])
    for cut in shards[1:]:
        level = level * one(*cut)
    return level


def noise(stream_key, shape, scale, most, cuts=(), held_as=jnp.bfloat16):
    level = steps_of(stream_key, shape, cuts, -0.22, 0.18) if cuts else 1.0
    result = jax.random.normal(stream_key, shape, jnp.float32) * scale * level
    return jnp.minimum(jnp.maximum(result, -most), most).astype(held_as)


def setup_inputs(seed: int = 0) -> dict:
    streams_of = jax.random.split(jax.random.key(seed), 9)
    return {
        "tokens": draw_tokens(jax.random.fold_in(streams_of[8], 71), 0),
        "grad_out": noise(streams_of[1], (TOKENS, D), 1.0, 6.0, ((0, 32), (1, 8))),
        "selected": draw_selected(jax.random.fold_in(streams_of[8], 71), 0),
        "gain": jnp.clip(1.0 + 0.18 * jax.random.normal(streams_of[3], (D,), jnp.float32), 0.1, 1.9),
        "router_weight": noise(streams_of[4], (D,), D ** -0.5, 0.0625, ((0, 8),), jnp.float32),
        "w_gate": noise(streams_of[5], (D, FF), D ** -0.5, 0.0625, ((0, 8), (1, 32))),
        "w_up": noise(streams_of[6], (D, FF), D ** -0.5, 0.0625, ((0, 8), (1, 32))),
        "w_down": noise(streams_of[7], (FF, D), FF ** -0.5, 0.03125, ((0, 32), (1, 8))),
    }


eps = 1e-06

def reference(tokens, grad_out, selected, gain, router_weight, w_gate, w_up, w_down):
    sel = tokens[selected]
    gsel = grad_out[selected]
    sel32 = sel.astype(jnp.float32)
    squares = lax.optimization_barrier(jnp.sum(sel32 * sel32, axis=1))
    logit = lax.optimization_barrier(jnp.sum(sel32 * router_weight[None, :], axis=1))
    scales = lax.rsqrt(squares / D + eps)
    normed = (sel32 * scales[:, None] * gain[None, :]).astype(jnp.bfloat16)
    gate = jnp.dot(normed, w_gate, preferred_element_type=jnp.float32)
    up = jnp.dot(normed, w_up, preferred_element_type=jnp.float32)
    sigma = jax.nn.sigmoid(gate)
    hidden = (gate * sigma * up).astype(jnp.bfloat16)
    back = jnp.dot(gsel, w_down.T, preferred_element_type=jnp.float32)
    router_grad = lax.optimization_barrier(jnp.sum(hidden.astype(jnp.float32) * back, axis=1))
    d_hidden = logit[:, None] * back
    d_gate = (d_hidden * up * (sigma + gate * sigma * (1.0 - sigma))).astype(jnp.bfloat16)
    d_up = (d_hidden * gate * sigma).astype(jnp.bfloat16)
    d_out = (logit[:, None] * gsel.astype(jnp.float32)).astype(jnp.bfloat16)
    grad_down = jnp.dot(hidden.T, d_out, preferred_element_type=jnp.float32).astype(jnp.bfloat16)
    grad_gate = jnp.dot(normed.T, d_gate, preferred_element_type=jnp.float32).astype(jnp.bfloat16)
    grad_up = jnp.dot(normed.T, d_up, preferred_element_type=jnp.float32).astype(jnp.bfloat16)
    d_normed = jnp.dot(d_gate, w_gate.T, preferred_element_type=jnp.float32) + jnp.dot(d_up, w_up.T, preferred_element_type=jnp.float32)
    grad_gain = lax.optimization_barrier(jnp.sum(d_normed * sel32 * scales[:, None], axis=0))
    dotted = lax.optimization_barrier(jnp.sum(gain[None, :] * d_normed * sel32, axis=1))
    cubed = scales * scales * scales
    d_sel = scales[:, None] * gain[None, :] * d_normed - sel32 * (cubed * dotted / D)[:, None] + router_grad[:, None] * router_weight[None, :]
    grad_x = grad_out.astype(jnp.float32).at[selected].add(d_sel).astype(jnp.bfloat16)
    grad_router = lax.optimization_barrier(jnp.sum(sel32 * router_grad[:, None], axis=0))
    return (grad_x, grad_gate, grad_up, grad_down, grad_gain, grad_router)
```

```python
import jax
import jax.numpy as jnp
from jax import lax
from jax.sharding import PartitionSpec as P

D = 8192
EPS = 1e-06
bf16 = jnp.bfloat16
f32 = jnp.float32
DOWN, UP = 2.0**-20, 2.0**20

WIDE = [(z, y, c) for z in range(8) for y in range(2) for c in range(2)]


def wide_pairs(move):
    def index(z, y, c):
        return (z % 8 * 2 + y) * 2 + c

    return [(index(*t), index(*move(*t))) for t in WIDE]


CORE = wide_pairs(lambda z, y, c: (z, y, 1 - c))
YLO = wide_pairs(lambda z, y, c: (z, 1 - y, c))
ZUP = wide_pairs(lambda z, y, c: (z + 1, y, c))
ZDOWN = wide_pairs(lambda z, y, c: (z + 7, y, c))
ZGROUPS = [[(z * 2 + y) * 2 + c for z in range(8)] for y in range(2) for c in range(2)]


def pieces(value, count):
    out = []
    for _ in range(count):
        head = lax.reduce_precision(value, 8, 7)
        out.append(head.astype(bf16))
        value = jnp.where(jnp.abs(head) < jnp.inf, value - head, 0.0)
    return out


def matmul(a, b, dims, out=f32):
    return lax.dot_general(a, b, (dims, ((), ())), preferred_element_type=out)


def local(tokens, grad_out, selected, gain, router_weight, w_gate, w_up, w_down):
    tok = tokens.shape[0]
    cap = tok // 4
    rows = selected.shape[0]
    w = lax.axis_index("wide")
    z, y, c = w // 4, (w // 2) % 2, w % 2

    def before(ids):
        return jnp.sum((selected[:, None] < ids[None, :]).astype(jnp.int32), axis=0)

    def slot_places(blocks):
        start, end = before(blocks * tok), before((blocks + 1) * tok)
        place = start[:, None] + jnp.arange(cap, dtype=jnp.int32)[None, :]
        return jnp.where(place < end[:, None], place, rows).reshape(-1)

    def onehot(places):
        return (places[:, None] == jnp.arange(rows, dtype=jnp.int32)[None, :]).astype(bf16)

    ids = w * tok + jnp.arange(tok, dtype=jnp.int32)
    first = before(w[None] * tok)
    rank = before(ids) - first
    marked = jnp.sum((selected[:, None] == ids[None, :]).astype(jnp.int32), axis=0) > 0
    pick = (
        (jnp.arange(cap, dtype=jnp.int32)[:, None] == rank[None, :]) & marked[None, :]
    ).astype(bf16)
    mine = jnp.concatenate(
        [
            matmul(pick, tokens, ((1,), (0,)), bf16),
            matmul(pick, grad_out, ((1,), (0,)), bf16),
        ],
        axis=0,
    )[None]

    base = jnp.concatenate([mine, lax.ppermute(mine, "wide", YLO)], axis=0)
    up = [base]
    down = [base]
    for _ in range(3):
        up.append(lax.ppermute(up[-1], "wide", ZUP))
        down.append(lax.ppermute(down[-1], "wide", ZDOWN))
    far_a = lax.ppermute(up[3][:1], "wide", ZUP)
    far_b = lax.ppermute(down[3][1:], "wide", ZDOWN)
    parts = [base] + up[1:] + down[1:] + [far_a, far_b]
    half = jnp.concatenate(parts, axis=0)
    other = lax.ppermute(half, "wide", CORE)
    steps = jnp.array([0, -1, -2, -3, 1, 2, 3, 4], jnp.int32)
    zs = (z + steps + 8) % 8
    chips = ((zs * 2)[:, None] + jnp.stack([y, 1 - y])[None, :]).reshape(-1) * 2
    put = onehot(slot_places(jnp.concatenate([chips + c, chips + 1 - c])))
    slots = jnp.concatenate([half, other], axis=0).reshape(32, 2, cap, -1)
    sel = matmul(put, slots[:, 0].reshape(32 * cap, -1), ((0,), (0,)), bf16)
    gsel = matmul(put, slots[:, 1].reshape(32 * cap, -1), ((0,), (0,)), bf16)

    sel32 = sel.astype(f32)
    squares = jnp.sum(sel32 * sel32, axis=1, keepdims=True)
    logit = jnp.sum(sel32 * router_weight[None, :], axis=1, keepdims=True)
    scaled = (sel32 * (gain * DOWN)[None, :]).astype(bf16)
    extra = jnp.concatenate(
        pieces(squares, 3) + pieces(logit, 3) + [jnp.zeros((rows, 122), bf16)], axis=1
    )
    send = jnp.concatenate(
        [
            matmul(scaled, w_gate, ((1,), (0,))).astype(bf16),
            matmul(scaled, w_up, ((1,), (0,))).astype(bf16),
            matmul(gsel, w_down, ((1,), (1,))).astype(bf16),
            extra,
        ],
        axis=1,
    ).reshape(8, rows // 8, -1)
    got = lax.all_to_all(send, "narrow", 0, 0, tiled=True)
    total = jnp.sum(got.astype(f32), axis=0)
    ff = w_gate.shape[1]
    tail = total[:, 3 * ff :]
    squares = jnp.sum(tail[:, 0:3], axis=1, keepdims=True)
    logit = jnp.sum(tail[:, 3:6], axis=1, keepdims=True)
    scale = lax.rsqrt(squares / D + EPS)
    gate = total[:, :ff] * (scale * UP)
    upv = total[:, ff : 2 * ff] * (scale * UP)
    back = total[:, 2 * ff : 3 * ff]
    sigma = jax.nn.sigmoid(gate)
    hidden = (gate * sigma * upv).astype(bf16)
    d_hidden = logit * back
    d_gate = (d_hidden * upv * (sigma + gate * sigma * (1.0 - sigma))).astype(bf16)
    d_up = (d_hidden * gate * sigma).astype(bf16)
    router_grad = jnp.sum(hidden.astype(f32) * back, axis=1, keepdims=True)
    inner = jnp.sum(d_gate.astype(f32) * gate + d_up.astype(f32) * upv, axis=1, keepdims=True)
    extra = jnp.concatenate(
        pieces(scale, 3)
        + pieces(logit, 3)
        + pieces(router_grad, 3)
        + pieces(inner, 3)
        + [jnp.zeros((rows // 8, 116), bf16)],
        axis=1,
    )
    share = jnp.concatenate([hidden, d_gate, d_up, extra], axis=1)
    gathered = lax.all_to_all(
        jnp.broadcast_to(share[None], (8,) + share.shape), "narrow", 0, 0, tiled=True
    ).reshape(rows, -1)
    hidden, d_gate, d_up = (gathered[:, k * ff : (k + 1) * ff] for k in range(3))
    tail = gathered[:, 3 * ff : 3 * ff + 12].astype(f32)
    scale, logit, router_grad, inner = (
        jnp.sum(tail[:, 3 * k : 3 * k + 3], axis=1, keepdims=True) for k in range(4)
    )

    d_normed = matmul(d_gate, w_gate, ((1,), (1,))) + matmul(d_up, w_up, ((1,), (1,)))
    small = jnp.concatenate(
        [
            jnp.sum(d_normed * sel32 * scale, axis=0, keepdims=True),
            jnp.sum(sel32 * router_grad, axis=0, keepdims=True),
            jnp.concatenate(
                [router_grad[:, 0], inner[:, 0], jnp.zeros((tokens.shape[1] - 2 * rows,), f32)]
            )[None],
        ],
        axis=0,
    )
    rounded = d_normed.astype(bf16)
    zy = jnp.arange(8, dtype=jnp.int32) * 2
    order = (jnp.stack([y, 1 - y])[:, None] + zy[None, :]).reshape(-1) * 2
    theirs = matmul(onehot(slot_places(order + 1 - c)), rounded, ((1,), (0,)), bf16)
    ours = matmul(onehot(slot_places(order + c)), rounded, ((1,), (0,)), bf16)
    part = ours.astype(f32) + lax.ppermute(theirs, "wide", CORE).astype(f32)
    small = small + lax.ppermute(small, "wide", CORE)
    part = part.reshape(2, 8, cap, -1)
    part = part[0] + lax.ppermute(part[1].astype(bf16), "wide", YLO).astype(f32)
    small = small + lax.ppermute(small, "wide", YLO)
    packed = jnp.concatenate(pieces(small, 2) + [jnp.zeros((2, small.shape[1]), bf16)], axis=0)
    message = jnp.concatenate(
        [part.astype(bf16), jnp.broadcast_to(packed[None], (8,) + packed.shape)], axis=1
    )
    message = lax.all_to_all(
        message, "wide", 0, 0, tiled=True, axis_index_groups=ZGROUPS
    )
    message = jnp.sum(message.astype(f32), axis=0)
    own = message[:cap]
    small = message[cap : cap + 3] + message[cap + 3 : cap + 6]

    normed = (sel32 * scale * gain[None, :]).astype(bf16)
    d_out = (logit * gsel.astype(f32)).astype(bf16)
    grad_down = matmul(hidden, d_out, ((0,), (0,))).astype(bf16)
    grad_gate = matmul(normed, d_gate, ((0,), (0,))).astype(bf16)
    grad_up = matmul(normed, d_up, ((0,), (0,))).astype(bf16)

    where = onehot(slot_places(w[None])).astype(f32)
    own_scale = jnp.sum(where * scale[:, 0][None, :], axis=1, keepdims=True)
    own_router = jnp.sum(where * small[2, :rows][None, :], axis=1, keepdims=True)
    own_inner = jnp.sum(where * small[2, rows : 2 * rows][None, :], axis=1, keepdims=True)
    own_sel = mine[0, :cap].astype(f32)
    d_sel = (
        own_scale * gain[None, :] * own
        - own_sel * (own_scale * own_scale * own_inner / D)
        + own_router * router_weight[None, :]
    )
    spread = lax.dot_general(
        pick.astype(f32), d_sel, (((0,), (0,)), ((), ())), precision=lax.Precision.HIGHEST
    )
    grad_x = (grad_out.astype(f32) + spread).astype(bf16)
    return (grad_x, grad_gate, grad_up, grad_down, small[0], small[1])


def solution(mesh):
    return jax.shard_map(
        local,
        mesh=mesh,
        in_specs=(
            P("wide", "narrow"),
            P("wide", "narrow"),
            P(),
            P("narrow"),
            P("narrow"),
            P("narrow", "wide"),
            P("narrow", "wide"),
            P("wide", "narrow"),
        ),
        out_specs=(
            P("wide", "narrow"),
            P("narrow", "wide"),
            P("narrow", "wide"),
            P("wide", "narrow"),
            P("narrow"),
            P("narrow"),
        ),
        check_vma=False,
    )
```

```python
import jax
import jax.numpy as jnp
import numpy as np
from jax import lax
from jax.experimental import pallas as pl
from jax.experimental.pallas import tpu as pltpu
from jax.sharding import PartitionSpec as P

D = 8192
EPS = 1e-06
bf16 = jnp.bfloat16
f32 = jnp.float32
i32 = jnp.int32
DOWN, UP = 2.0**-20, 2.0**20
TOK = 96
CAP = 24
SEL = 384
W = 1024
TILE = 256

WIDE = [(z, y, c) for z in range(8) for y in range(2) for c in range(2)]


def wide_pairs(move):
    def index(z, y, c):
        return (z % 8 * 2 + y) * 2 + c

    return [(index(*t), index(*move(*t))) for t in WIDE]


CORE = wide_pairs(lambda z, y, c: (z, y, 1 - c))
YLO = wide_pairs(lambda z, y, c: (z, 1 - y, c))
ZUP = wide_pairs(lambda z, y, c: (z + 1, y, c))
ZDOWN = wide_pairs(lambda z, y, c: (z + 7, y, c))
ZFAR = wide_pairs(lambda z, y, c: (z + 1 + 6 * c, y, c))
ZGROUPS = [[(z * 2 + y) * 2 + c for z in range(8)] for y in range(2) for c in range(2)]

GATHER = np.zeros((8, 768), np.int32)
_s = np.arange(768)
GATHER[0] = _s // 48 % 8 - 3
GATHER[1] = _s // 24 % 2
GATHER[2] = _s // 384
GATHER[3] = _s % 24
SPREAD = np.zeros((8, 768), np.int32)
SPREAD[0] = _s // 24 % 8
SPREAD[1] = _s // 192 % 2
SPREAD[2] = 1 - _s // 384
SPREAD[3] = _s % 24

VMEM = pl.BlockSpec(memory_space=pltpu.VMEM)


def params(mib=48):
    return pltpu.CompilerParams(vmem_limit_bytes=mib << 20)


def cost(flops, bytes_):
    return pl.CostEstimate(flops=int(flops), bytes_accessed=int(bytes_), transcendentals=0)


def pieces(value, count):
    out = []
    for _ in range(count):
        head = lax.reduce_precision(value, 8, 7)
        out.append(head.astype(bf16))
        value = jnp.where(jnp.abs(head) < jnp.inf, value - head, 0.0)
    return out


def heads(value, count):
    out = []
    for _ in range(count):
        head = value.astype(bf16).astype(f32)
        out.append(head)
        value = jnp.where(jnp.abs(head) < jnp.inf, value - head, 0.0)
    return out


def lanes_of(columns, rows):
    lane = lax.broadcasted_iota(i32, (rows, 128), 1)
    out = jnp.zeros((rows, 128), f32)
    for k, column in enumerate(columns):
        out = jnp.where(lane == k, column, out)
    return out.astype(bf16)


def mm(a, b, ca, cb):
    return lax.dot_general(a, b, (((ca,), (cb,)), ((), ())), preferred_element_type=f32)


def place_of():
    w = lax.axis_index("wide")
    return w, w // 4, (w // 2) % 2, w % 2


def count_before(sel_col, ids):
    return jnp.sum(jnp.where(sel_col < ids, 1, 0).astype(i32), axis=0, keepdims=True)


def placement(sel_col, z, y, c, zz, yrel, crel, k):
    block = zz * 4 + (y ^ yrel) * 2 + (c ^ crel)
    start = count_before(sel_col, block * TOK)
    end = count_before(sel_col, block * TOK + TOK)
    row = lax.broadcasted_iota(i32, (SEL, k.shape[1]), 0)
    return jnp.where((row == start + k) & (row < end), 1.0, 0.0).astype(bf16)


def pick_of(sel_col, w):
    ids = w * TOK + lax.broadcasted_iota(i32, (1, TOK), 1)
    first = count_before(sel_col, jnp.full((1, 1), w * TOK, i32))
    last = count_before(sel_col, jnp.full((1, 1), w * TOK + TOK, i32))
    rank = count_before(sel_col, ids) - first
    marked = jnp.sum(jnp.where(sel_col == ids, 1, 0).astype(i32), axis=0, keepdims=True) > 0
    k = lax.broadcasted_iota(i32, (CAP, TOK), 0)
    return jnp.where((k == rank) & marked, 1.0, 0.0), first, last


def own_kernel(sel_ref, tok_ref, go_ref, x_ref, g_ref):
    w, _, _, _ = place_of()
    pick = pick_of(sel_ref[...], w)[0].astype(bf16)
    x_ref[...] = mm(pick, tok_ref[...], 1, 0).astype(bf16)
    g_ref[...] = mm(pick, go_ref[...], 1, 0).astype(bf16)


def gate_kernel(*refs):
    pieces_in = refs[:16]
    table, sel_col, gain, rw, wg, wu, put, sel, out, slots, scaled = refs[16:]
    j = pl.program_id(0)

    @pl.when(j == 0)
    def _():
        _, z, y, c = place_of()
        t = table[...]
        zz = (z + t[0:1] + 8) & 7
        put[...] = placement(sel_col[...], z, y, c, zz, t[1:2], t[2:3], t[3:4])
        for p in range(16):
            slots[48 * p : 48 * p + 48, :] = pieces_in[p][...]
        squares = jnp.zeros((SEL, 1), f32)
        logit = jnp.zeros((SEL, 1), f32)
        for k in range(W // TILE):
            cols = slice(k * TILE, (k + 1) * TILE)
            tile = mm(put[...], slots[:, cols], 1, 0)
            sel[:, cols] = tile.astype(bf16)
            squares += jnp.sum(tile * tile, axis=1, keepdims=True)
            logit += jnp.sum(tile * rw[:, cols], axis=1, keepdims=True)
            scaled[:, cols] = (tile * (gain[:, cols] * DOWN)).astype(bf16)
        out[:, 2 * W :] = lanes_of(heads(squares, 3) + heads(logit, 3), SEL)

    at = pl.multiple_of(j * TILE, TILE)
    out[:, pl.ds(at, TILE)] = mm(scaled[...], wg[...], 1, 0).astype(bf16)
    out[:, pl.ds(pl.multiple_of(W + j * TILE, TILE), TILE)] = mm(
        scaled[...], wu[...], 1, 0
    ).astype(bf16)


def back_kernel(*refs):
    pieces_in = refs[:16]
    put, wd, gsel, out, slots = refs[16:]
    j = pl.program_id(0)

    @pl.when(j == 0)
    def _():
        for p in range(16):
            slots[48 * p : 48 * p + 48, :] = pieces_in[p][...]
        for k in range(W // TILE):
            cols = slice(k * TILE, (k + 1) * TILE)
            gsel[:, cols] = mm(put[...], slots[:, cols], 1, 0).astype(bf16)

    out[...] = mm(gsel[...], wd[...], 1, 1).astype(bf16)


def hidden_kernel(gu, bk, d_out, h_out):
    rows = SEL // 8
    tail = jnp.sum(gu[:, :, 2 * W :].astype(f32), axis=0)
    squares = tail[:, 0:1] + tail[:, 1:2] + tail[:, 2:3]
    logit = tail[:, 3:4] + tail[:, 4:5] + tail[:, 5:6]
    scale = lax.rsqrt(squares / D + EPS)
    router_grad = jnp.zeros((rows, 1), f32)
    inner = jnp.zeros((rows, 1), f32)
    for k in range(W // TILE):
        lo, hi = k * TILE, (k + 1) * TILE
        gate = jnp.sum(gu[:, :, lo:hi].astype(f32), axis=0) * (scale * UP)
        upv = jnp.sum(gu[:, :, W + lo : W + hi].astype(f32), axis=0) * (scale * UP)
        back = jnp.sum(bk[:, :, lo:hi].astype(f32), axis=0)
        sigma = jax.nn.sigmoid(gate)
        hidden = (gate * sigma * upv).astype(bf16)
        d_hidden = logit * back
        d_gate = (d_hidden * upv * (sigma + gate * sigma * (1.0 - sigma))).astype(bf16)
        d_up = (d_hidden * gate * sigma).astype(bf16)
        router_grad += jnp.sum(hidden.astype(f32) * back, axis=1, keepdims=True)
        inner += jnp.sum(
            d_gate.astype(f32) * gate + d_up.astype(f32) * upv, axis=1, keepdims=True
        )
        for n in range(8):
            d_out[n, :, lo:hi] = d_gate
            d_out[n, :, W + lo : W + hi] = d_up
            h_out[n, :, lo:hi] = hidden
    extra = lanes_of(
        heads(scale, 3) + heads(logit, 3) + heads(router_grad, 3) + heads(inner, 3), rows
    )
    for n in range(8):
        d_out[n, :, 2 * W :] = extra


def to_row(column):
    eye = lax.broadcasted_iota(i32, (SEL, SEL), 0) == lax.broadcasted_iota(i32, (SEL, SEL), 1)
    return jnp.sum(jnp.where(eye, column, 0.0), axis=0, keepdims=True)


def normed_kernel(table, sel_col, gd, wg, wu, sel, theirs, ours, small, put, cols):
    j = pl.program_id(0)

    @pl.when(j == 0)
    def _():
        _, z, y, c = place_of()
        t = table[...]
        put[...] = placement(sel_col[...], z, y, c, t[0:1], t[1:2], t[2:3], t[3:4])
        tail = gd[:, 2 * W :].astype(f32)
        lane = lax.broadcasted_iota(i32, (SEL, 128), 1)

        def value(k):
            return jnp.sum(
                jnp.where((lane >= 3 * k) & (lane < 3 * k + 3), tail, 0.0), axis=1, keepdims=True
            )

        scale, router_grad, inner = value(0), value(2), value(3)
        cols[...] = jnp.where(lane == 0, scale, router_grad)
        small[...] = jnp.zeros(small.shape, f32)
        small[2:3, 0:SEL] = to_row(router_grad)
        small[2:3, SEL : 2 * SEL] = to_row(inner)
        small[3:4, 0:SEL] = to_row(scale)

    part = mm(gd[:, 0:W], wg[...], 1, 1) + mm(gd[:, W : 2 * W], wu[...], 1, 1)
    sel32 = sel[...].astype(f32)
    at = pl.ds(pl.multiple_of(j * TILE, TILE), TILE)
    small[0:1, at] = jnp.sum(part * sel32 * cols[:, 0:1], axis=0, keepdims=True)
    small[1:2, at] = jnp.sum(sel32 * cols[:, 1:2], axis=0, keepdims=True)
    rounded = part.astype(bf16)
    both = mm(put[...], rounded, 0, 0).astype(bf16)
    theirs[...] = both[:SEL]
    ours[...] = both[SEL:]


def final_kernel(msg, x, go, gain, rw, sel_col, small, grad_x, out_small):
    w, _, _, _ = place_of()
    pick, first, last = pick_of(sel_col[...], w)
    total = jnp.sum(msg[...].astype(f32), axis=0)
    summed = total[CAP : CAP + 3] + total[CAP + 3 : CAP + 6]
    out_small[...] = summed
    own = total[:CAP]
    row = lax.broadcasted_iota(i32, (CAP, SEL), 1)
    k = lax.broadcasted_iota(i32, (CAP, SEL), 0)
    where = (row == first + k) & (row < last)

    def mine(values):
        return jnp.sum(jnp.where(where, values, 0.0), axis=1, keepdims=True)

    scale = mine(small[3:4, 0:SEL])
    router_grad = mine(summed[2:3, 0:SEL])
    inner = mine(summed[2:3, SEL : 2 * SEL])
    d_sel = (
        scale * gain[...] * own
        - x[...].astype(f32) * (scale * scale * inner / D)
        + router_grad * rw[...]
    )
    spread = jnp.zeros((TOK, W), f32)
    for piece in heads(d_sel, 3):
        spread += mm(pick.astype(bf16), piece.astype(bf16), 0, 0)
    grad_x[...] = (go[...].astype(f32) + spread).astype(bf16)


def gather(mine):
    pair = jnp.concatenate([mine, lax.ppermute(mine, "wide", YLO)], axis=0)
    held = {0: pair}
    for k in range(1, 4):
        held[-k] = lax.ppermute(held[1 - k], "wide", ZUP)
        held[k] = lax.ppermute(held[k - 1], "wide", ZDOWN)
    core = lax.axis_index("wide") % 2
    held[4] = lax.ppermute(jnp.where(core == 0, held[-3], held[3]), "wide", ZFAR)
    ours = [held[k] for k in range(-3, 5)]
    return ours + [lax.ppermute(piece, "wide", CORE) for piece in ours]


def local(tokens, grad_out, selected, gain, router_weight, w_gate, w_up, w_down):
    sel_col = selected.reshape(SEL, 1)
    gain = gain.reshape(1, W)
    router_weight = router_weight.reshape(1, W)
    slot = jax.ShapeDtypeStruct((CAP, W), bf16)
    x, g = pl.pallas_call(
        own_kernel,
        out_shape=(slot, slot),
        in_specs=[VMEM] * 3,
        out_specs=(VMEM, VMEM),
        compiler_params=params(16),
        name="own",
    )(sel_col, tokens, grad_out)
    xs = gather(x)
    gs = gather(g)

    full = lambda *shape: pl.BlockSpec(shape, lambda j: (0,) * len(shape))
    put, sel, send = pl.pallas_call(
        gate_kernel,
        grid=(W // TILE,),
        out_shape=(
            jax.ShapeDtypeStruct((SEL, 768), bf16),
            jax.ShapeDtypeStruct((SEL, W), bf16),
            jax.ShapeDtypeStruct((SEL, 2 * W + 128), bf16),
        ),
        in_specs=[full(48, W)] * 16
        + [full(8, 768), full(SEL, 1), full(1, W), full(1, W)]
        + [pl.BlockSpec((W, TILE), lambda j: (0, j))] * 2,
        out_specs=(full(SEL, 768), full(SEL, W), full(SEL, 2 * W + 128)),
        scratch_shapes=[pltpu.VMEM((768, W), bf16), pltpu.VMEM((SEL, W), bf16)],
        compiler_params=params(),
        cost_estimate=cost(2.2e9, 9e6),
        name="gate_up",
    )(*xs, jnp.asarray(GATHER), sel_col, gain, router_weight, w_gate, w_up)
    got_gu = lax.all_to_all(send.reshape(8, SEL // 8, -1), "narrow", 0, 0, tiled=True)
    gsel, send = pl.pallas_call(
        back_kernel,
        grid=(W // TILE,),
        out_shape=(
            jax.ShapeDtypeStruct((SEL, W), bf16),
            jax.ShapeDtypeStruct((SEL, W), bf16),
        ),
        in_specs=[full(48, W)] * 16
        + [full(SEL, 768), pl.BlockSpec((TILE, W), lambda j: (j, 0))],
        out_specs=(full(SEL, W), pl.BlockSpec((SEL, TILE), lambda j: (0, j))),
        scratch_shapes=[pltpu.VMEM((768, W), bf16)],
        compiler_params=params(),
        cost_estimate=cost(1.4e9, 6e6),
        name="back",
    )(*gs, put, w_down)
    got_b = lax.all_to_all(send.reshape(8, SEL // 8, -1), "narrow", 0, 0, tiled=True)

    share_d, share_h = pl.pallas_call(
        hidden_kernel,
        out_shape=(
            jax.ShapeDtypeStruct((8, SEL // 8, 2 * W + 128), bf16),
            jax.ShapeDtypeStruct((8, SEL // 8, W), bf16),
        ),
        in_specs=[VMEM, VMEM],
        out_specs=(VMEM, VMEM),
        compiler_params=params(),
        name="hidden",
    )(got_gu, got_b)
    gd = lax.all_to_all(share_d, "narrow", 0, 0, tiled=True).reshape(SEL, -1)
    gd, share_h = lax.optimization_barrier((gd, share_h))
    hidden = lax.all_to_all(share_h, "narrow", 0, 0, tiled=True).reshape(SEL, W)

    theirs, ours, small = pl.pallas_call(
        normed_kernel,
        grid=(W // TILE,),
        out_shape=(
            jax.ShapeDtypeStruct((SEL, W), bf16),
            jax.ShapeDtypeStruct((SEL, W), bf16),
            jax.ShapeDtypeStruct((8, W), f32),
        ),
        in_specs=[full(8, 768), full(SEL, 1), full(SEL, 2 * W + 128)]
        + [pl.BlockSpec((TILE, W), lambda j: (j, 0))] * 2
        + [pl.BlockSpec((SEL, TILE), lambda j: (0, j))],
        out_specs=(
            pl.BlockSpec((SEL, TILE), lambda j: (0, j)),
            pl.BlockSpec((SEL, TILE), lambda j: (0, j)),
            full(8, W),
        ),
        scratch_shapes=[pltpu.VMEM((SEL, 768), bf16), pltpu.VMEM((SEL, 128), f32)],
        compiler_params=params(),
        cost_estimate=cost(2.4e9, 9e6),
        name="normed",
    )(jnp.asarray(SPREAD), sel_col, gd, w_gate, w_up, sel)

    total = small[:3]
    part = ours.astype(f32) + lax.ppermute(theirs, "wide", CORE).astype(f32)
    total = total + lax.ppermute(total, "wide", CORE)
    part = part.reshape(2, 8, CAP, W)
    part = part[0] + lax.ppermute(part[1].astype(bf16), "wide", YLO).astype(f32)
    total = total + lax.ppermute(total, "wide", YLO)
    packed = jnp.concatenate(pieces(total, 2) + [jnp.zeros((2, W), bf16)], axis=0)
    message = jnp.concatenate(
        [part.astype(bf16), jnp.broadcast_to(packed[None], (8,) + packed.shape)], axis=1
    )
    message = lax.all_to_all(
        message, "wide", 0, 0, tiled=True, axis_index_groups=ZGROUPS
    )

    tail = gd[:, 2 * W :].astype(f32)
    scale = jnp.sum(tail[:, 0:3], axis=1, keepdims=True)
    logit = jnp.sum(tail[:, 3:6], axis=1, keepdims=True)
    normed = (sel.astype(f32) * scale * gain).astype(bf16)
    d_out = (logit * gsel.astype(f32)).astype(bf16)
    grad_gate = mm(normed, gd[:, :W], 0, 0).astype(bf16)
    grad_up = mm(normed, gd[:, W : 2 * W], 0, 0).astype(bf16)
    grad_down = mm(hidden, d_out, 0, 0).astype(bf16)

    grad_x, total = pl.pallas_call(
        final_kernel,
        out_shape=(
            jax.ShapeDtypeStruct((TOK, W), bf16),
            jax.ShapeDtypeStruct((3, W), f32),
        ),
        in_specs=[VMEM] * 7,
        out_specs=(VMEM, VMEM),
        compiler_params=params(16),
        name="final",
    )(message, x, grad_out, gain, router_weight, sel_col, small)
    return (grad_x, grad_gate, grad_up, grad_down, total[0], total[1])


def solution(mesh):
    return jax.shard_map(
        local,
        mesh=mesh,
        in_specs=(
            P("wide", "narrow"),
            P("wide", "narrow"),
            P(),
            P("narrow"),
            P("narrow"),
            P("narrow", "wide"),
            P("narrow", "wide"),
            P("wide", "narrow"),
        ),
        out_specs=(
            P("wide", "narrow"),
            P("narrow", "wide"),
            P("narrow", "wide"),
            P("wide", "narrow"),
            P("narrow"),
            P("narrow"),
        ),
        check_vma=False,
    )
```

```python
import jax
import jax.numpy as jnp
from jax import lax
from jax.experimental import pallas as pl
from jax.experimental.pallas import tpu as pltpu
from jax.sharding import PartitionSpec as P

D = 8192
EPS = 1e-06
bf16 = jnp.bfloat16
f32 = jnp.float32
i32 = jnp.int32
DOWN, UP = 2.0**-20, 2.0**20
TOK = 96
CAP = 24
SEL = 384
W = 1024
TILE = 256

WIDE = [(z, y, c) for z in range(8) for y in range(2) for c in range(2)]


def wide_pairs(move):
    def index(z, y, c):
        return (z % 8 * 2 + y) * 2 + c

    return [(index(*t), index(*move(*t))) for t in WIDE]


CORE = wide_pairs(lambda z, y, c: (z, y, 1 - c))
YLO = wide_pairs(lambda z, y, c: (z, 1 - y, c))
ZFAR = wide_pairs(lambda z, y, c: (z + 2 + 4 * c, y, c))


def along(value, step):
    return lax.ppermute(value, "wide", wide_pairs(lambda z, y, c: (z + 8 + step, y, c)))


VMEM = pl.BlockSpec(memory_space=pltpu.VMEM)


def params(mib=24):
    return pltpu.CompilerParams(vmem_limit_bytes=mib << 20)


def cost(flops, bytes_):
    return pl.CostEstimate(flops=int(flops), bytes_accessed=int(bytes_), transcendentals=0)


def heads(value, count):
    out = []
    for _ in range(count):
        head = value.astype(bf16).astype(f32)
        out.append(head)
        value = jnp.where(jnp.abs(head) < jnp.inf, value - head, 0.0)
    return out


def lanes_of(columns, rows):
    lane = lax.broadcasted_iota(i32, (rows, 128), 1)
    out = jnp.zeros((rows, 128), f32)
    for k, column in enumerate(columns):
        out = jnp.where(lane == k, column, out)
    return out.astype(bf16)


def mm(a, b, ca, cb):
    return lax.dot_general(a, b, (((ca,), (cb,)), ((), ())), preferred_element_type=f32)


def place_of():
    w = lax.axis_index("wide")
    return w, w // 4, (w // 2) % 2, w % 2


def count_before(sel_col, ids):
    return jnp.sum(jnp.where(sel_col < ids, 1, 0).astype(i32), axis=0, keepdims=True)


def placement(sel_col):
    _, z, y, c = place_of()
    slot = lax.broadcasted_iota(i32, (1, 2 * SEL), 1)
    n = (slot * 2731) >> 16
    k = slot - n * CAP
    zz = (z + ((n >> 1) & 7) + 5) & 7
    block = zz * 4 + (y ^ (n & 1)) * 2 + (c ^ (n >> 4))
    start = count_before(sel_col, block * TOK)
    end = count_before(sel_col, block * TOK + TOK)
    row = lax.broadcasted_iota(i32, (SEL, 2 * SEL), 0)
    return jnp.where((row == start + k) & (row < end), 1.0, 0.0)


def pick_of(sel_row):
    w, _, _, _ = place_of()

    def before(ids):
        return jnp.sum(jnp.where(sel_row < ids, 1, 0).astype(i32), axis=1, keepdims=True)

    ids = w * TOK + lax.broadcasted_iota(i32, (TOK, 1), 0)
    first = before(jnp.full((1, 1), w * TOK, i32))
    last = before(jnp.full((1, 1), w * TOK + TOK, i32))
    rank = before(ids) - first
    marked = before(ids + 1) - before(ids) > 0
    k = lax.broadcasted_iota(i32, (TOK, CAP), 1)
    return jnp.where((k == rank) & marked, 1.0, 0.0).astype(bf16), first, last


def own_kernel(sel_hbm, tok_hbm, go_hbm, out, row, sel, tok, go, sems):
    copies = [
        pltpu.make_async_copy(tok_hbm, tok, sems.at[0]),
        pltpu.make_async_copy(go_hbm, go, sems.at[1]),
        pltpu.make_async_copy(sel_hbm, sel, sems.at[2]),
    ]
    for copy in copies:
        copy.start()
    copies[2].wait()
    sel_row = sel[...].reshape(1, SEL)
    row[...] = sel_row
    pick = pick_of(sel_row)[0]
    for n, held in enumerate((tok, go)):
        copies[n].wait()
        out[n] = mm(pick, held[...], 0, 0).astype(bf16)


def base_kernel(mine, other, out):
    parts = [mine[0], other[0], mine[1], other[1]]
    out[...] = jnp.concatenate([part.astype(f32) for part in parts], axis=0).astype(bf16)


def onehot_kernel(sel_col, gain, rw, _, put, spread, vectors):
    vectors[0:1, :] = gain[...]
    vectors[1:2, :] = rw[...]
    hot = placement(sel_col[...])
    put[...] = hot.astype(bf16)
    spread[...] = hot.T.astype(bf16)


def forward_kernel(*refs):
    parts = refs[:16]
    put, vectors, wg, wu, wd, sel, gsel, out, slots, scaled = refs[16:]
    j = pl.program_id(0)

    @pl.when(j == 0)
    def _():
        for p in range(16):
            slots[48 * p : 48 * p + 48, 0:W] = parts[p][0:48, :]
            slots[48 * p : 48 * p + 48, W : 2 * W] = parts[p][48:96, :]
        squares = jnp.zeros((SEL, 1), f32)
        logit = jnp.zeros((SEL, 1), f32)
        for k in range(W // TILE):
            cols = slice(k * TILE, (k + 1) * TILE)
            tile = mm(put[...], slots[:, cols], 1, 0)
            sel[:, cols] = tile.astype(bf16)
            squares += jnp.sum(tile * tile, axis=1, keepdims=True)
            logit += jnp.sum(tile * vectors[1:2, cols], axis=1, keepdims=True)
            scaled[:, cols] = (tile * (vectors[0:1, cols] * DOWN)).astype(bf16)
            tile = mm(put[...], slots[:, W + k * TILE : W + (k + 1) * TILE], 1, 0)
            gsel[:, cols] = tile.astype(bf16)
        out[:, 3 * W :] = lanes_of(heads(squares, 3) + heads(logit, 3), SEL)

    def at(start):
        return pl.ds(pl.multiple_of(start + j * TILE, TILE), TILE)

    out[:, at(0)] = mm(scaled[...], wg[...], 1, 0).astype(bf16)
    out[:, at(W)] = mm(scaled[...], wu[...], 1, 0).astype(bf16)
    out[:, at(2 * W)] = mm(gsel[...], wd[...], 1, 1).astype(bf16)


def hidden_kernel(got, d_out, h_out):
    rows = SEL // 8

    def total(lo, hi):
        return jnp.sum(got[:, :, lo:hi].astype(f32), axis=0)

    tail = total(3 * W, 3 * W + 128)
    squares = tail[:, 0:1] + tail[:, 1:2] + tail[:, 2:3]
    logit = tail[:, 3:4] + tail[:, 4:5] + tail[:, 5:6]
    scale = lax.rsqrt(squares / D + EPS)
    router_grad = jnp.zeros((rows, 1), f32)
    inner = jnp.zeros((rows, 1), f32)
    for k in range(W // TILE):
        lo, hi = k * TILE, (k + 1) * TILE
        gate = total(lo, hi) * (scale * UP)
        upv = total(W + lo, W + hi) * (scale * UP)
        back = total(2 * W + lo, 2 * W + hi)
        sigma = jax.nn.sigmoid(gate)
        hidden = (gate * sigma * upv).astype(bf16)
        d_hidden = logit * back
        d_gate = (d_hidden * upv * (sigma + gate * sigma * (1.0 - sigma))).astype(bf16)
        d_up = (d_hidden * gate * sigma).astype(bf16)
        router_grad += jnp.sum(hidden.astype(f32) * back, axis=1, keepdims=True)
        inner += jnp.sum(
            d_gate.astype(f32) * gate + d_up.astype(f32) * upv, axis=1, keepdims=True
        )
        for n in range(8):
            d_out[n, :, lo:hi] = d_gate
            d_out[n, :, W + lo : W + hi] = d_up
            h_out[n, :, lo:hi] = hidden
    extra = lanes_of(
        heads(scale, 3) + heads(logit, 3) + heads(router_grad, 3) + heads(inner, 3), rows
    )
    for n in range(8):
        d_out[n, :, 2 * W :] = extra


def with_small(rows, small):
    return jnp.concatenate([rows] + heads(small, 2), axis=0).astype(bf16)


def apart(ref):
    value = ref[...].astype(f32)
    n = value.shape[0] - 8
    return value[:n], value[n : n + 4] + value[n + 4 : n + 8]


def to_row(column):
    eye = lax.broadcasted_iota(i32, (SEL, SEL), 0) == lax.broadcasted_iota(i32, (SEL, SEL), 1)
    return jnp.sum(jnp.where(eye, column, 0.0), axis=0, keepdims=True)


def normed_kernel(spread, gd, wg, wu, sel, theirs, ours, small, cols):
    j = pl.program_id(0)

    @pl.when(j == 0)
    def _():
        tail = gd[:, 2 * W :].astype(f32)
        lane = lax.broadcasted_iota(i32, (SEL, 128), 1)

        def value(k):
            return jnp.sum(
                jnp.where((lane >= 3 * k) & (lane < 3 * k + 3), tail, 0.0), axis=1, keepdims=True
            )

        scale, router_grad, inner = value(0), value(2), value(3)
        cols[...] = jnp.where(lane == 0, scale, router_grad)
        small[...] = jnp.zeros(small.shape, f32)
        small[2:3, 0:SEL] = to_row(router_grad)
        small[2:3, SEL : 2 * SEL] = to_row(inner)
        small[3:4, 0:SEL] = to_row(scale)

    part = mm(gd[:, 0:W], wg[...], 1, 1) + mm(gd[:, W : 2 * W], wu[...], 1, 1)
    sel32 = sel[...].astype(f32)
    at = pl.ds(pl.multiple_of(j * TILE, TILE), TILE)
    small[0:1, at] = jnp.sum(part * sel32 * cols[:, 0:1], axis=0, keepdims=True)
    small[1:2, at] = jnp.sum(sel32 * cols[:, 1:2], axis=0, keepdims=True)
    rounded = part.astype(bf16)
    ours[...] = mm(spread[:SEL, :], rounded, 1, 0).astype(bf16)
    theirs[...] = with_small(mm(spread[SEL:, :], rounded, 1, 0), small[0:4, at])


def join_kernel(ours, theirs, mine, up3, down3, far, up1, down1, small):
    rows, other = apart(theirs)
    total = mine[0:4, :] + other
    small[...] = total
    for n, out in ((0, down3), (2, down1), (4, up1), (6, up3), (7, far)):
        at = slice(48 * n, 48 * n + 48)
        out[...] = with_small(ours[at, :].astype(f32) + rows[at], total)


def relay_kernel(
    up2, up2_other, from_below, down2, down2_other, from_above, far, small, to_up, to_down
):
    _, _, _, c = place_of()
    rows, one = apart(far)
    for base, other, ref, mask, out in (
        (up2, up2_other, from_below, c == 0, to_up),
        (down2, down2_other, from_above, c == 1, to_down),
    ):
        chunk, two = apart(ref)
        out[...] = with_small(
            base[...].astype(f32) + other[...].astype(f32) + chunk + jnp.where(mask, rows, 0.0),
            small[...] + two + jnp.where(mask, one, 0.0),
        )


def pair_kernel(stay, stay_other, small, a, b, c, d, here, there):
    total, low = stay[...].astype(f32) + stay_other[...].astype(f32), small[...]
    for part in (a, b, c, d):
        rows, other = apart(part)
        total, low = total + rows, low + other
    here[0:CAP, :] = total[:CAP]
    here[CAP : CAP + 4, :] = low
    there[...] = with_small(total[CAP:], low)


def far_kernel(below, above, _, out):
    out[...] = jnp.where(place_of()[3] == 0, below[...], above[...])


def final_kernel(here, there, mine, go, vectors, sel_row, small, grad_x, d_gain, d_router):
    pick, first, last = pick_of(sel_row[...])
    rows, summed = apart(there)
    own = here[0:CAP, :] + rows
    summed = summed + here[CAP : CAP + 4, :]
    d_gain[...] = summed[0:1]
    d_router[...] = summed[1:2]
    row = lax.broadcasted_iota(i32, (CAP, SEL), 1)
    k = lax.broadcasted_iota(i32, (CAP, SEL), 0)
    where = (row == first + k) & (row < last)

    def place(values):
        return jnp.sum(jnp.where(where, values, 0.0), axis=1, keepdims=True)

    scale = place(small[3:4, 0:SEL])
    router_grad = place(summed[2:3, 0:SEL])
    inner = place(summed[2:3, SEL : 2 * SEL])
    d_sel = (
        scale * vectors[0:1, :] * own
        - mine[0].astype(f32) * (scale * scale * inner / D)
        + router_grad * vectors[1:2, :]
    )
    spread = jnp.zeros((TOK, W), f32)
    for piece in heads(d_sel, 3):
        spread += mm(pick, piece.astype(bf16), 1, 0)
    grad_x[...] = (go[...].astype(f32) + spread).astype(bf16)


def gather(pair, after):
    held = {0: pair}
    for k in (2, 1):
        held[-k] = along(pair, k)
        held[k] = along(pair, -k)
    held[-3] = along(held[-2], 1)
    held[3] = along(held[2], -1)
    far = pl.pallas_call(
        far_kernel,
        out_shape=jax.ShapeDtypeStruct(pair.shape, bf16),
        in_specs=[VMEM] * 2 + [pl.BlockSpec(memory_space=pl.ANY)],
        out_specs=VMEM,
        compiler_params=params(16),
        name="far",
    )(held[-2], held[2], after)
    held[4] = lax.ppermute(far, "wide", ZFAR)
    ours = [held[k] for k in range(-3, 5)]
    return ours + [lax.ppermute(piece, "wide", CORE) for piece in ours]


def local(tokens, grad_out, selected, gain, router_weight, w_gate, w_up, w_down):
    sel_col = selected.reshape(SEL, 1)
    gain = gain.reshape(1, W)
    router_weight = router_weight.reshape(1, W)
    anywhere = pl.BlockSpec(memory_space=pl.ANY)
    mine, sel_row = pl.pallas_call(
        own_kernel,
        out_shape=(
            jax.ShapeDtypeStruct((2, CAP, W), bf16),
            jax.ShapeDtypeStruct((1, SEL), i32),
        ),
        in_specs=[anywhere] * 3,
        out_specs=(VMEM, VMEM),
        scratch_shapes=[pltpu.VMEM((SEL,), i32)]
        + [pltpu.VMEM((TOK, W), bf16)] * 2
        + [pltpu.SemaphoreType.DMA((3,))],
        compiler_params=params(60),
        name="own",
    )(selected, tokens, grad_out)
    put, spread, vectors = pl.pallas_call(
        onehot_kernel,
        out_shape=(
            jax.ShapeDtypeStruct((SEL, 2 * SEL), bf16),
            jax.ShapeDtypeStruct((2 * SEL, SEL), bf16),
            jax.ShapeDtypeStruct((2, W), f32),
        ),
        in_specs=[VMEM] * 3 + [pl.BlockSpec(memory_space=pl.ANY)],
        out_specs=(VMEM,) * 3,
        compiler_params=params(24),
        name="onehot",
    )(sel_col, gain, router_weight, mine)
    pair = pl.pallas_call(
        base_kernel,
        out_shape=jax.ShapeDtypeStruct((4 * CAP, W), bf16),
        in_specs=[VMEM] * 2,
        out_specs=VMEM,
        compiler_params=params(16),
        name="base",
    )(mine, lax.ppermute(mine, "wide", YLO))
    parts = gather(pair, put)

    full = lambda *shape: pl.BlockSpec(shape, lambda j: (0,) * len(shape))
    sel, gsel, send = pl.pallas_call(
        forward_kernel,
        grid=(W // TILE,),
        out_shape=(
            jax.ShapeDtypeStruct((SEL, W), bf16),
            jax.ShapeDtypeStruct((SEL, W), bf16),
            jax.ShapeDtypeStruct((SEL, 3 * W + 128), bf16),
        ),
        in_specs=[full(96, W)] * 16
        + [full(SEL, 768), full(2, W)]
        + [pl.BlockSpec((W, TILE), lambda j: (0, j))] * 2
        + [pl.BlockSpec((TILE, W), lambda j: (j, 0))],
        out_specs=(full(SEL, W), full(SEL, W), full(SEL, 3 * W + 128)),
        scratch_shapes=[pltpu.VMEM((768, 2 * W), bf16), pltpu.VMEM((SEL, W), bf16)],
        compiler_params=params(48),
        cost_estimate=cost(3.6e9, 16e6),
        name="forward",
    )(*parts, put, vectors, w_gate, w_up, w_down)
    got = lax.all_to_all(send.reshape(8, SEL // 8, -1), "narrow", 0, 0, tiled=True)

    share_d, share_h = pl.pallas_call(
        hidden_kernel,
        out_shape=(
            jax.ShapeDtypeStruct((8, SEL // 8, 2 * W + 128), bf16),
            jax.ShapeDtypeStruct((8, SEL // 8, W), bf16),
        ),
        in_specs=[VMEM],
        out_specs=(VMEM, VMEM),
        compiler_params=params(),
        name="hidden",
    )(got)
    gd = lax.all_to_all(share_d, "narrow", 0, 0, tiled=True).reshape(SEL, -1)
    gd, share_h = lax.optimization_barrier((gd, share_h))
    hidden = lax.all_to_all(share_h, "narrow", 0, 0, tiled=True).reshape(SEL, W)

    theirs, ours, small = pl.pallas_call(
        normed_kernel,
        grid=(W // TILE,),
        out_shape=(
            jax.ShapeDtypeStruct((SEL + 8, W), bf16),
            jax.ShapeDtypeStruct((SEL, W), bf16),
            jax.ShapeDtypeStruct((8, W), f32),
        ),
        in_specs=[full(768, SEL), full(SEL, 2 * W + 128)]
        + [pl.BlockSpec((TILE, W), lambda j: (j, 0))] * 2
        + [pl.BlockSpec((SEL, TILE), lambda j: (0, j))],
        out_specs=(
            pl.BlockSpec((SEL + 8, TILE), lambda j: (0, j)),
            pl.BlockSpec((SEL, TILE), lambda j: (0, j)),
            full(8, W),
        ),
        scratch_shapes=[pltpu.VMEM((SEL, 128), f32)],
        compiler_params=params(),
        cost_estimate=cost(2.4e9, 9e6),
        name="normed",
    )(spread, gd, w_gate, w_up, sel)

    part = jax.ShapeDtypeStruct((56, W), bf16)
    theirs = lax.ppermute(theirs, "wide", CORE)
    up3, down3, far, up1, down1, total = pl.pallas_call(
        join_kernel,
        out_shape=(part,) * 5 + (jax.ShapeDtypeStruct((4, W), f32),),
        in_specs=[VMEM] * 3,
        out_specs=(VMEM,) * 6,
        compiler_params=params(16),
        name="join",
    )(ours, theirs, small)
    from_below, from_above = along(up3, 1), along(down3, -1)
    far = lax.ppermute(far, "wide", ZFAR)
    near = along(up1, 1), along(down1, -1)

    def chunk(n):
        return pl.BlockSpec((48, W), lambda j: (n, 0))

    up2, down2 = pl.pallas_call(
        relay_kernel,
        grid=(1,),
        out_shape=(part, part),
        in_specs=[chunk(5), chunk(5), full(56, W), chunk(1), chunk(1)]
        + [full(56, W), full(56, W), full(4, W)],
        out_specs=(full(56, W), full(56, W)),
        compiler_params=params(16),
        name="relay",
    )(ours, theirs, from_below, ours, theirs, from_above, far, total)
    here, there = pl.pallas_call(
        pair_kernel,
        grid=(1,),
        out_shape=(
            jax.ShapeDtypeStruct((CAP + 4, W), f32),
            jax.ShapeDtypeStruct((CAP + 8, W), bf16),
        ),
        in_specs=[chunk(3), chunk(3), full(4, W)] + [full(56, W)] * 4,
        out_specs=(full(CAP + 4, W), full(CAP + 8, W)),
        compiler_params=params(16),
        name="pair",
    )(ours, theirs, total, *near, along(up2, 2), along(down2, -2))
    there = lax.ppermute(there, "wide", YLO)

    tail = gd[:, 2 * W :].astype(f32)
    scale = jnp.sum(tail[:, 0:3], axis=1, keepdims=True)
    logit = jnp.sum(tail[:, 3:6], axis=1, keepdims=True)
    normed = (sel.astype(f32) * scale * gain).astype(bf16)
    d_out = (logit * gsel.astype(f32)).astype(bf16)
    grad_gate = mm(normed, gd[:, :W], 0, 0).astype(bf16)
    grad_up = mm(normed, gd[:, W : 2 * W], 0, 0).astype(bf16)
    grad_down = mm(hidden, d_out, 0, 0).astype(bf16)

    vector = jax.ShapeDtypeStruct((1, W), f32)
    grad_x, d_gain, d_router = pl.pallas_call(
        final_kernel,
        out_shape=(jax.ShapeDtypeStruct((TOK, W), bf16), vector, vector),
        in_specs=[VMEM] * 7,
        out_specs=(VMEM,) * 3,
        compiler_params=params(16),
        name="final",
    )(here, there, mine, grad_out, vectors, sel_row, small)
    return (grad_x, grad_gate, grad_up, grad_down, d_gain.reshape(W), d_router.reshape(W))


def solution(mesh):
    return jax.shard_map(
        local,
        mesh=mesh,
        in_specs=(
            P("wide", "narrow"),
            P("wide", "narrow"),
            P(),
            P("narrow"),
            P("narrow"),
            P("narrow", "wide"),
            P("narrow", "wide"),
            P("wide", "narrow"),
        ),
        out_specs=(
            P("wide", "narrow"),
            P("narrow", "wide"),
            P("narrow", "wide"),
            P("wide", "narrow"),
            P("narrow"),
            P("narrow"),
        ),
        check_vma=False,
    )
```

```python
import jax
import jax.numpy as jnp
from jax import lax
from jax.experimental import pallas as pl
from jax.experimental.pallas import tpu as pltpu
from jax.sharding import PartitionSpec as P

D = 8192
EPS = 1e-06
bf16 = jnp.bfloat16
f32 = jnp.float32
i32 = jnp.int32
DOWN, UP = 2.0**-20, 2.0**20
TOK = 96
CAP = 24
SEL = 384
W = 1024
TILE = 256

WIDE = [(z, y, c) for z in range(8) for y in range(2) for c in range(2)]


def wide_pairs(move):
    def index(z, y, c):
        return (z % 8 * 2 + y) * 2 + c

    return [(index(*t), index(*move(*t))) for t in WIDE]


CORE = wide_pairs(lambda z, y, c: (z, y, 1 - c))
YLO = wide_pairs(lambda z, y, c: (z, 1 - y, c))
XUP = [(n, n // 4 * 4 + (n + 1) % 4) for n in range(8)]
XDOWN = [(n, n // 4 * 4 + (n + 3) % 4) for n in range(8)]
XFAR = [(n, n // 4 * 4 + (n + 2) % 4) for n in range(8)]
YHI = [(n, (n + 4) % 8) for n in range(8)]
ROW = 3 * 1024 + 128
ZFAR = wide_pairs(lambda z, y, c: (z + 2 + 4 * c, y, c))


def along(value, step):
    return lax.ppermute(value, "wide", wide_pairs(lambda z, y, c: (z + 8 + step, y, c)))


VMEM = pl.BlockSpec(memory_space=pltpu.VMEM)


def params(mib=24):
    return pltpu.CompilerParams(vmem_limit_bytes=mib << 20)


def cost(flops, bytes_):
    return pl.CostEstimate(flops=int(flops), bytes_accessed=int(bytes_), transcendentals=0)


def heads(value, count):
    out = []
    for _ in range(count):
        head = value.astype(bf16).astype(f32)
        out.append(head)
        value = jnp.where(jnp.abs(head) < jnp.inf, value - head, 0.0)
    return out


def lanes_of(columns, rows):
    lane = lax.broadcasted_iota(i32, (rows, 128), 1)
    out = jnp.zeros((rows, 128), f32)
    for k, column in enumerate(columns):
        out = jnp.where(lane == k, column, out)
    return out.astype(bf16)


def mm(a, b, ca, cb):
    return lax.dot_general(a, b, (((ca,), (cb,)), ((), ())), preferred_element_type=f32)


def place_of():
    w = lax.axis_index("wide")
    return w, w // 4, (w // 2) % 2, w % 2


def count_before(sel_col, ids):
    return jnp.sum(jnp.where(sel_col < ids, 1, 0).astype(i32), axis=0, keepdims=True)


def compact_of(i):
    n = lax.axis_index("narrow")
    r = (i * 1366) >> 16
    block = (r & 4 ^ n & 4) | ((r + n) & 3)
    return i + (block - r) * 48


def placement(sel_col):
    _, z, y, c = place_of()
    slot = lax.broadcasted_iota(i32, (1, 2 * SEL), 1)
    n = (slot * 2731) >> 16
    k = slot - n * CAP
    zz = (z + ((n >> 1) & 7) + 5) & 7
    block = zz * 4 + (y ^ (n & 1)) * 2 + (c ^ (n >> 4))
    start = count_before(sel_col, block * TOK)
    end = count_before(sel_col, block * TOK + TOK)
    row = compact_of(lax.broadcasted_iota(i32, (SEL, 1), 0))
    return jnp.where((row == start + k) & (row < end), 1.0, 0.0)


def pick_of(sel_row):
    w, _, _, _ = place_of()

    def before(ids):
        return jnp.sum(jnp.where(sel_row < ids, 1, 0).astype(i32), axis=1, keepdims=True)

    ids = w * TOK + lax.broadcasted_iota(i32, (TOK, 1), 0)
    first = before(jnp.full((1, 1), w * TOK, i32))
    last = before(jnp.full((1, 1), w * TOK + TOK, i32))
    rank = before(ids) - first
    marked = before(ids + 1) - before(ids) > 0
    k = lax.broadcasted_iota(i32, (TOK, CAP), 1)
    return jnp.where((k == rank) & marked, 1.0, 0.0).astype(bf16), first, last


def own_kernel(sel_hbm, tok_hbm, go_hbm, out, row, sel, tok, go, sems):
    copies = [
        pltpu.make_async_copy(tok_hbm, tok, sems.at[0]),
        pltpu.make_async_copy(go_hbm, go, sems.at[1]),
        pltpu.make_async_copy(sel_hbm, sel, sems.at[2]),
    ]
    for copy in copies:
        copy.start()
    copies[2].wait()
    sel_row = sel[...].reshape(1, SEL)
    row[...] = sel_row
    pick = pick_of(sel_row)[0]
    for n, held in enumerate((tok, go)):
        copies[n].wait()
        out[:, n * W : n * W + W] = mm(pick, held[...], 0, 0).astype(bf16)


def onehot_kernel(sel_col, gain, rw, _, put, spread, vectors):
    vectors[0:1, :] = gain[...]
    vectors[1:2, :] = rw[...]
    hot = placement(sel_col[...])
    put[...] = hot.astype(bf16)
    spread[...] = hot.T.astype(bf16)


def forward_kernel(*refs):
    parts = refs[:16]
    put, vectors, wg, wu, wd, sel, gsel, keep, to_up, to_down, to_y, slots, scaled = refs[16:]
    j = pl.program_id(0)

    def write(cols, value):
        value = value.astype(bf16)
        for r, (out, at) in enumerate(
            (
                (keep, 0),
                (to_up, 48),
                (keep, 96),
                (to_down, 48),
                (keep, 48),
                (to_up, 0),
                (to_y, 0),
                (to_down, 0),
            )
        ):
            out[at : at + 48, cols] = value[48 * r : 48 * r + 48]

    @pl.when(j == 0)
    def _():
        for p in range(16):
            slots[48 * p : 48 * p + 48, :] = parts[p][...]
        squares = jnp.zeros((SEL, 128), f32)
        logit = jnp.zeros((SEL, 128), f32)
        for k in range(W // TILE):
            cols = slice(k * TILE, (k + 1) * TILE)
            tile = mm(put[...], slots[:, cols], 1, 0)
            sel[:, cols] = tile.astype(bf16)
            for m in range(TILE // 128):
                lanes = tile[:, 128 * m : 128 * m + 128]
                squares += lanes * lanes
                logit += lanes * vectors[1:2, k * TILE + 128 * m : k * TILE + 128 * m + 128]
            scaled[:, cols] = (tile * (vectors[0:1, cols] * DOWN)).astype(bf16)
            tile = mm(put[...], slots[:, W + k * TILE : W + (k + 1) * TILE], 1, 0)
            gsel[:, cols] = tile.astype(bf16)
        squares = jnp.sum(squares, axis=1, keepdims=True)
        logit = jnp.sum(logit, axis=1, keepdims=True)
        write(slice(3 * W, ROW), lanes_of(heads(squares, 3) + heads(logit, 3), SEL))

    def at(start):
        return pl.ds(pl.multiple_of(start + j * TILE, TILE), TILE)

    write(at(0), mm(scaled[...], wg[...], 1, 0))
    write(at(W), mm(scaled[...], wu[...], 1, 0))
    write(at(2 * W), mm(gsel[...], wd[...], 1, 1))


def stats(refs):
    tail = 0.0
    for ref in refs:
        tail = tail + ref[:, 3 * W :].astype(f32)
    return (
        tail[:, 0:1] + tail[:, 1:2] + tail[:, 2:3],
        tail[:, 3:4] + tail[:, 4:5] + tail[:, 5:6],
    )


def sum_kernel(keep, from_below, from_above, from_y, to_y, to_far):
    for out, refs in (
        (to_y, (keep.at[48:96], from_below.at[0:48], from_above.at[0:48])),
        (to_far, (keep.at[96:144], from_y)),
    ):
        for k in range(3 * W // TILE):
            cols = slice(k * TILE, (k + 1) * TILE)
            total = refs[0][:, cols].astype(f32)
            for ref in refs[1:]:
                total = total + ref[:, cols].astype(f32)
            out[:, cols] = total.astype(bf16)
        squares, logit = stats(refs)
        out[:, 3 * W :] = lanes_of(heads(squares, 3) + heads(logit, 3), SEL // 8)


def hidden_kernel(keep, from_below, from_above, from_y, from_far, out):
    rows = SEL // 8
    refs = (keep.at[0:48], from_below.at[48:96], from_above.at[48:96], from_y, from_far)

    def total(start):
        value = refs[0][:, start : start + TILE].astype(f32)
        for ref in refs[1:]:
            value = value + ref[:, start : start + TILE].astype(f32)
        return value

    squares, logit = stats(refs)
    scale = lax.rsqrt(squares / D + EPS)
    router_grad = jnp.zeros((rows, 1), f32)
    inner = jnp.zeros((rows, 1), f32)
    for lo in range(0, W, TILE):
        gate = total(lo) * (scale * UP)
        upv = total(W + lo) * (scale * UP)
        back = total(2 * W + lo)
        sigma = jax.nn.sigmoid(gate)
        hidden = (gate * sigma * upv).astype(bf16)
        d_hidden = logit * back
        d_gate = (d_hidden * upv * (sigma + gate * sigma * (1.0 - sigma))).astype(bf16)
        d_up = (d_hidden * gate * sigma).astype(bf16)
        router_grad += jnp.sum(hidden.astype(f32) * back, axis=1, keepdims=True)
        inner += jnp.sum(
            d_gate.astype(f32) * gate + d_up.astype(f32) * upv, axis=1, keepdims=True
        )
        out[:, lo : lo + TILE] = d_gate
        out[:, W + lo : W + lo + TILE] = d_up
        out[:, 2 * W + lo : 2 * W + lo + TILE] = hidden
    out[:, 3 * W :] = lanes_of(
        heads(scale, 3) + heads(logit, 3) + heads(router_grad, 3) + heads(inner, 3), rows
    )


def with_small(rows, small):
    return jnp.concatenate([rows] + heads(small, 2), axis=0).astype(bf16)


def apart(ref):
    value = ref[...].astype(f32)
    n = value.shape[0] - 8
    return value[:n], value[n : n + 4] + value[n + 4 : n + 8]


def to_row(column):
    eye = lax.broadcasted_iota(i32, (SEL, SEL), 0) == lax.broadcasted_iota(i32, (SEL, SEL), 1)
    return jnp.sum(jnp.where(eye, column, 0.0), axis=0, keepdims=True)


def normed_kernel(
    spread, own, above, b2, below, b4, b6, wg, wu, sel, theirs, ours, small, gd, cols
):
    j = pl.program_id(0)

    @pl.when(j == 0)
    def _():
        tail = []
        for r, (ref, at) in enumerate(
            (
                (own, 0),
                (above, 0),
                (b2, 0),
                (below, 0),
                (b4, 0),
                (above, 48),
                (b6, 0),
                (below, 48),
            )
        ):
            gd[48 * r : 48 * r + 48, :] = ref[at : at + 48, 0 : 2 * W]
            tail.append(ref[at : at + 48, 3 * W :].astype(f32))
        tail = jnp.concatenate(tail, axis=0)
        lane = lax.broadcasted_iota(i32, (SEL, 128), 1)

        def value(k):
            return jnp.sum(
                jnp.where((lane >= 3 * k) & (lane < 3 * k + 3), tail, 0.0), axis=1, keepdims=True
            )

        scale, router_grad, inner = value(0), value(2), value(3)
        cols[...] = jnp.where(lane == 0, scale, router_grad)
        small[...] = jnp.zeros(small.shape, f32)
        small[2:3, 0:SEL] = to_row(router_grad)
        small[2:3, SEL : 2 * SEL] = to_row(inner)
        small[3:4, 0:SEL] = to_row(scale)

    part = mm(gd[:, 0:W], wg[...], 1, 1) + mm(gd[:, W : 2 * W], wu[...], 1, 1)
    sel32 = sel[...].astype(f32)
    at = pl.ds(pl.multiple_of(j * TILE, TILE), TILE)
    small[0:1, at] = jnp.sum(part * sel32 * cols[:, 0:1], axis=0, keepdims=True)
    small[1:2, at] = jnp.sum(sel32 * cols[:, 1:2], axis=0, keepdims=True)
    rounded = part.astype(bf16)
    ours[...] = mm(spread[:SEL, :], rounded, 1, 0).astype(bf16)
    theirs[...] = with_small(mm(spread[SEL:, :], rounded, 1, 0), small[0:4, at])


def join_kernel(ours, theirs, mine, up3, down3, far, up1, down1, small):
    rows, other = apart(theirs)
    total = mine[0:4, :] + other
    small[...] = total
    for n, out in ((0, down3), (2, down1), (4, up1), (6, up3), (7, far)):
        at = slice(48 * n, 48 * n + 48)
        out[...] = with_small(ours[at, :].astype(f32) + rows[at], total)


def relay_kernel(
    up2, up2_other, from_below, down2, down2_other, from_above, far, small, to_up, to_down
):
    _, _, _, c = place_of()
    rows, one = apart(far)
    for base, other, ref, mask, out in (
        (up2, up2_other, from_below, c == 0, to_up),
        (down2, down2_other, from_above, c == 1, to_down),
    ):
        chunk, two = apart(ref)
        out[...] = with_small(
            base[...].astype(f32) + other[...].astype(f32) + chunk + jnp.where(mask, rows, 0.0),
            small[...] + two + jnp.where(mask, one, 0.0),
        )


def pair_kernel(stay, stay_other, small, a, b, c, d, here, there):
    total, low = stay[...].astype(f32) + stay_other[...].astype(f32), small[...]
    for part in (a, b, c, d):
        rows, other = apart(part)
        total, low = total + rows, low + other
    here[0:CAP, :] = total[:CAP]
    here[CAP : CAP + 4, :] = low
    there[...] = with_small(total[CAP:], low)


def far_kernel(below, above, _, out):
    out[...] = jnp.where(place_of()[3] == 0, below[...], above[...])


def final_kernel(here, there, mine, go, vectors, sel_row, small, grad_x, d_gain, d_router):
    pick, first, last = pick_of(sel_row[...])
    rows, summed = apart(there)
    own = here[0:CAP, :] + rows
    summed = summed + here[CAP : CAP + 4, :]
    d_gain[...] = summed[0:1]
    d_router[...] = summed[1:2]
    row = compact_of(lax.broadcasted_iota(i32, (1, SEL), 1))
    k = lax.broadcasted_iota(i32, (CAP, SEL), 0)
    where = (row == first + k) & (row < last)

    def place(values):
        return jnp.sum(jnp.where(where, values, 0.0), axis=1, keepdims=True)

    scale = place(small[3:4, 0:SEL])
    router_grad = place(summed[2:3, 0:SEL])
    inner = place(summed[2:3, SEL : 2 * SEL])
    d_sel = (
        scale * vectors[0:1, :] * own
        - mine[:, 0:W].astype(f32) * (scale * scale * inner / D)
        + router_grad * vectors[1:2, :]
    )
    spread = jnp.zeros((TOK, W), f32)
    for piece in heads(d_sel, 3):
        spread += mm(pick, piece.astype(bf16), 1, 0)
    grad_x[...] = (go[...].astype(f32) + spread).astype(bf16)


def gather(pair, after):
    held = {0: pair}
    for k in (2, 1):
        held[-k] = along(pair, k)
        held[k] = along(pair, -k)
    held[-3] = along(held[-2], 1)
    held[3] = along(held[2], -1)
    far = pl.pallas_call(
        far_kernel,
        out_shape=jax.ShapeDtypeStruct(pair.shape, bf16),
        in_specs=[VMEM] * 2 + [pl.BlockSpec(memory_space=pl.ANY)],
        out_specs=VMEM,
        compiler_params=params(16),
        name="far",
    )(held[-2], held[2], after)
    held[4] = lax.ppermute(far, "wide", ZFAR)
    ours = [held[k] for k in range(-3, 5)]
    return ours + [lax.ppermute(piece, "wide", CORE) for piece in ours]


def local(tokens, grad_out, selected, gain, router_weight, w_gate, w_up, w_down):
    sel_col = selected.reshape(SEL, 1)
    gain = gain.reshape(1, W)
    router_weight = router_weight.reshape(1, W)
    anywhere = pl.BlockSpec(memory_space=pl.ANY)
    mine, sel_row = pl.pallas_call(
        own_kernel,
        out_shape=(
            jax.ShapeDtypeStruct((CAP, 2 * W), bf16),
            jax.ShapeDtypeStruct((1, SEL), i32),
        ),
        in_specs=[anywhere] * 3,
        out_specs=(VMEM, VMEM),
        scratch_shapes=[pltpu.VMEM((SEL,), i32)]
        + [pltpu.VMEM((TOK, W), bf16)] * 2
        + [pltpu.SemaphoreType.DMA((3,))],
        compiler_params=params(60),
        name="own",
    )(selected, tokens, grad_out)
    put, spread, vectors = pl.pallas_call(
        onehot_kernel,
        out_shape=(
            jax.ShapeDtypeStruct((SEL, 2 * SEL), bf16),
            jax.ShapeDtypeStruct((2 * SEL, SEL), bf16),
            jax.ShapeDtypeStruct((2, W), f32),
        ),
        in_specs=[VMEM] * 3 + [pl.BlockSpec(memory_space=pl.ANY)],
        out_specs=(VMEM,) * 3,
        compiler_params=params(24),
        name="onehot",
    )(sel_col, gain, router_weight, mine)
    pair = jnp.concatenate([mine, lax.ppermute(mine, "wide", YLO)], axis=0)
    parts = gather(pair, put)

    full = lambda *shape: pl.BlockSpec(shape, lambda j: (0,) * len(shape))
    block = jax.ShapeDtypeStruct((48, ROW), bf16)
    blocks = jax.ShapeDtypeStruct((96, ROW), bf16)
    sel, gsel, keep, to_up, to_down, to_y = pl.pallas_call(
        forward_kernel,
        grid=(W // TILE,),
        out_shape=(
            jax.ShapeDtypeStruct((SEL, W), bf16),
            jax.ShapeDtypeStruct((SEL, W), bf16),
            jax.ShapeDtypeStruct((144, ROW), bf16),
            blocks,
            blocks,
            block,
        ),
        in_specs=[full(48, 2 * W)] * 16
        + [full(SEL, 768), full(2, W)]
        + [pl.BlockSpec((W, TILE), lambda j: (0, j))] * 2
        + [pl.BlockSpec((TILE, W), lambda j: (j, 0))],
        out_specs=(full(SEL, W), full(SEL, W), full(144, ROW))
        + (full(96, ROW), full(96, ROW), full(48, ROW)),
        scratch_shapes=[pltpu.VMEM((768, 2 * W), bf16), pltpu.VMEM((SEL, W), bf16)],
        compiler_params=params(48),
        cost_estimate=cost(3.6e9, 16e6),
        name="forward",
    )(*parts, put, vectors, w_gate, w_up, w_down)

    from_below = lax.ppermute(to_up, "narrow", XUP)
    from_above = lax.ppermute(to_down, "narrow", XDOWN)
    from_y = lax.ppermute(to_y, "narrow", YHI)
    to_y, to_far = pl.pallas_call(
        sum_kernel,
        out_shape=(block, block),
        in_specs=[VMEM] * 4,
        out_specs=(VMEM, VMEM),
        compiler_params=params(),
        name="sum",
    )(keep, from_below, from_above, from_y)
    from_far = lax.ppermute(to_far, "narrow", XFAR)
    from_y = lax.ppermute(to_y, "narrow", YHI)
    own = pl.pallas_call(
        hidden_kernel,
        out_shape=block,
        in_specs=[VMEM] * 5,
        out_specs=VMEM,
        compiler_params=params(),
        name="hidden",
    )(keep, from_below, from_above, from_y, from_far)

    b2 = lax.ppermute(own, "narrow", XFAR)
    b4 = lax.ppermute(own, "narrow", YHI)
    column = jnp.concatenate([own, b4], axis=0)
    below = lax.ppermute(column, "narrow", XUP)
    above = lax.ppermute(column, "narrow", XDOWN)
    b6 = lax.ppermute(b2, "narrow", YHI)

    theirs, ours, small = pl.pallas_call(
        normed_kernel,
        grid=(W // TILE,),
        out_shape=(
            jax.ShapeDtypeStruct((SEL + 8, W), bf16),
            jax.ShapeDtypeStruct((SEL, W), bf16),
            jax.ShapeDtypeStruct((8, W), f32),
        ),
        in_specs=[full(768, SEL), full(48, ROW), full(96, ROW), full(48, ROW), full(96, ROW)]
        + [full(48, ROW)] * 2
        + [pl.BlockSpec((TILE, W), lambda j: (j, 0))] * 2
        + [pl.BlockSpec((SEL, TILE), lambda j: (0, j))],
        out_specs=(
            pl.BlockSpec((SEL + 8, TILE), lambda j: (0, j)),
            pl.BlockSpec((SEL, TILE), lambda j: (0, j)),
            full(8, W),
        ),
        scratch_shapes=[pltpu.VMEM((SEL, 2 * W), bf16), pltpu.VMEM((SEL, 128), f32)],
        compiler_params=params(),
        cost_estimate=cost(2.4e9, 9e6),
        name="normed",
    )(spread, own, above, b2, below, b4, b6, w_gate, w_up, sel)

    part = jax.ShapeDtypeStruct((56, W), bf16)
    theirs = lax.ppermute(theirs, "wide", CORE)
    up3, down3, far, up1, down1, total = pl.pallas_call(
        join_kernel,
        out_shape=(part,) * 5 + (jax.ShapeDtypeStruct((4, W), f32),),
        in_specs=[VMEM] * 3,
        out_specs=(VMEM,) * 6,
        compiler_params=params(16),
        name="join",
    )(ours, theirs, small)
    from_below, from_above = along(up3, 1), along(down3, -1)
    far = lax.ppermute(far, "wide", ZFAR)
    near = along(up1, 1), along(down1, -1)

    def chunk(n):
        return pl.BlockSpec((48, W), lambda j: (n, 0))

    up2, down2 = pl.pallas_call(
        relay_kernel,
        grid=(1,),
        out_shape=(part, part),
        in_specs=[chunk(5), chunk(5), full(56, W), chunk(1), chunk(1)]
        + [full(56, W), full(56, W), full(4, W)],
        out_specs=(full(56, W), full(56, W)),
        compiler_params=params(16),
        name="relay",
    )(ours, theirs, from_below, ours, theirs, from_above, far, total)
    here, there = pl.pallas_call(
        pair_kernel,
        grid=(1,),
        out_shape=(
            jax.ShapeDtypeStruct((CAP + 4, W), f32),
            jax.ShapeDtypeStruct((CAP + 8, W), bf16),
        ),
        in_specs=[chunk(3), chunk(3), full(4, W)] + [full(56, W)] * 4,
        out_specs=(full(CAP + 4, W), full(CAP + 8, W)),
        compiler_params=params(16),
        name="pair",
    )(ours, theirs, total, *near, along(up2, 2), along(down2, -2))
    there = lax.ppermute(there, "wide", YLO)

    rows = jnp.concatenate([own, above[:48], b2, below[:48], b4, above[48:], b6, below[48:]])
    tail = rows[:, 3 * W :].astype(f32)
    scale = jnp.sum(tail[:, 0:3], axis=1, keepdims=True)
    logit = jnp.sum(tail[:, 3:6], axis=1, keepdims=True)
    normed = (sel.astype(f32) * scale * gain).astype(bf16)
    d_out = (logit * gsel.astype(f32)).astype(bf16)
    grad_gate = mm(normed, rows[:, :W], 0, 0).astype(bf16)
    grad_up = mm(normed, rows[:, W : 2 * W], 0, 0).astype(bf16)
    grad_down = mm(rows[:, 2 * W : 3 * W], d_out, 0, 0).astype(bf16)

    vector = jax.ShapeDtypeStruct((1, W), f32)
    grad_x, d_gain, d_router = pl.pallas_call(
        final_kernel,
        out_shape=(jax.ShapeDtypeStruct((TOK, W), bf16), vector, vector),
        in_specs=[VMEM] * 7,
        out_specs=(VMEM,) * 3,
        compiler_params=params(16),
        name="final",
    )(here, there, mine, grad_out, vectors, sel_row, small)
    return (grad_x, grad_gate, grad_up, grad_down, d_gain.reshape(W), d_router.reshape(W))


def solution(mesh):
    return jax.shard_map(
        local,
        mesh=mesh,
        in_specs=(
            P("wide", "narrow"),
            P("wide", "narrow"),
            P(),
            P("narrow"),
            P("narrow"),
            P("narrow", "wide"),
            P("narrow", "wide"),
            P("wide", "narrow"),
        ),
        out_specs=(
            P("wide", "narrow"),
            P("narrow", "wide"),
            P("narrow", "wide"),
            P("wide", "narrow"),
            P("narrow"),
            P("narrow"),
        ),
        check_vma=False,
    )
```

```python
import jax
import jax.numpy as jnp
from jax import lax
from jax.experimental import pallas as pl
from jax.experimental.pallas import tpu as pltpu
from jax.sharding import PartitionSpec as P

D = 8192
EPS = 1e-06
bf16 = jnp.bfloat16
f32 = jnp.float32
i32 = jnp.int32
DOWN, UP = 2.0**-20, 2.0**20
TOK = 96
CAP = 24
SEL = 384
W = 1024
TILE = 256
WIDER = 512

WIDE = [(z, y, c) for z in range(8) for y in range(2) for c in range(2)]


def wide_pairs(move):
    def index(z, y, c):
        return (z % 8 * 2 + y) * 2 + c

    return [(index(*t), index(*move(*t))) for t in WIDE]


CORE = wide_pairs(lambda z, y, c: (z, y, 1 - c))
YLO = wide_pairs(lambda z, y, c: (z, 1 - y, c))
XUP = [(n, n // 4 * 4 + (n + 1) % 4) for n in range(8)]
XDOWN = [(n, n // 4 * 4 + (n + 3) % 4) for n in range(8)]
XFAR = [(n, n // 4 * 4 + (n + 2) % 4) for n in range(8)]
YHI = [(n, (n + 4) % 8) for n in range(8)]
ROW = 3 * 1024 + 128
ZFAR = wide_pairs(lambda z, y, c: (z + 2 + 4 * c, y, c))


def along(value, step):
    return lax.ppermute(value, "wide", wide_pairs(lambda z, y, c: (z + 8 + step, y, c)))


VMEM = pl.BlockSpec(memory_space=pltpu.VMEM)


def params(mib=24):
    return pltpu.CompilerParams(vmem_limit_bytes=mib << 20)


def cost(flops, bytes_):
    return pl.CostEstimate(flops=int(flops), bytes_accessed=int(bytes_), transcendentals=0)


def heads(value, count):
    out = []
    for _ in range(count):
        head = value.astype(bf16).astype(f32)
        out.append(head)
        value = jnp.where(jnp.abs(head) < jnp.inf, value - head, 0.0)
    return out


def lanes_of(columns, rows):
    lane = lax.broadcasted_iota(i32, (rows, 128), 1)
    out = jnp.zeros((rows, 128), f32)
    for k, column in enumerate(columns):
        out = jnp.where(lane == k, column, out)
    return out.astype(bf16)


def mm(a, b, ca, cb):
    return lax.dot_general(a, b, (((ca,), (cb,)), ((), ())), preferred_element_type=f32)


def place_of():
    w = lax.axis_index("wide")
    return w, w // 4, (w // 2) % 2, w % 2


def count_before(sel_col, ids):
    return jnp.sum(jnp.where(sel_col < ids, 1, 0).astype(i32), axis=0, keepdims=True)


def compact_of(i):
    n = lax.axis_index("narrow")
    r = (i * 1366) >> 16
    block = (r & 4 ^ n & 4) | ((r + n) & 3)
    return i + (block - r) * 48


def placement(sel_col):
    _, z, y, c = place_of()
    slot = lax.broadcasted_iota(i32, (1, 2 * SEL), 1)
    n = (slot * 2731) >> 16
    k = slot - n * CAP
    zz = (z + ((n >> 1) & 7) + 5) & 7
    block = zz * 4 + (y ^ (n & 1)) * 2 + (c ^ (n >> 4))
    start = count_before(sel_col, block * TOK)
    end = count_before(sel_col, block * TOK + TOK)
    row = compact_of(lax.broadcasted_iota(i32, (SEL, 1), 0))
    return jnp.where((row == start + k) & (row < end), 1.0, 0.0)


def pick_of(sel_row):
    w, _, _, _ = place_of()

    def before(ids):
        return jnp.sum(jnp.where(sel_row < ids, 1, 0).astype(i32), axis=1, keepdims=True)

    ids = w * TOK + lax.broadcasted_iota(i32, (TOK, 1), 0)
    first = before(jnp.full((1, 1), w * TOK, i32))
    last = before(jnp.full((1, 1), w * TOK + TOK, i32))
    rank = before(ids) - first
    marked = before(ids + 1) - before(ids) > 0
    k = lax.broadcasted_iota(i32, (TOK, CAP), 1)
    return jnp.where((k == rank) & marked, 1.0, 0.0).astype(bf16), first, last


def own_kernel(sel_hbm, tok_hbm, go_hbm, out, row, sel, tok, go, sems):
    copies = [
        pltpu.make_async_copy(tok_hbm, tok, sems.at[0]),
        pltpu.make_async_copy(go_hbm, go, sems.at[1]),
        pltpu.make_async_copy(sel_hbm, sel, sems.at[2]),
    ]
    for copy in copies:
        copy.start()
    copies[2].wait()
    sel_row = sel[...].reshape(1, SEL)
    row[...] = sel_row
    pick = pick_of(sel_row)[0]
    for n, held in enumerate((tok, go)):
        copies[n].wait()
        out[:, n * W : n * W + W] = mm(pick, held[...], 0, 0).astype(bf16)


def onehot_kernel(sel_col, gain, rw, _, *refs):
    weights, (put, spread, vectors), held, sems = refs[:3], refs[3:6], refs[6:9], refs[9]
    loads = [pltpu.make_async_copy(weights[n], held[n], sems.at[n]) for n in range(3)]
    for load in loads:
        load.start()
    vectors[0:1, :] = gain[...]
    vectors[1:2, :] = rw[...]
    hot = placement(sel_col[...])
    put[...] = hot.astype(bf16)
    spread[...] = hot.T.astype(bf16)
    for load in loads:
        load.wait()


def forward_kernel(*refs):
    parts = refs[:16]
    put, vectors, *held, sel, gsel, keep = refs[16:24]
    to_up, to_down, to_y, near_up, near_down, slots, scaled = refs[24:]

    def write(lo, hi, value):
        value = value.astype(bf16)
        for r, (out, at) in enumerate(
            (
                (keep, 0),
                (near_up, 0),
                (keep, 96),
                (near_down, 0),
                (keep, 48),
                (to_up, 0),
                (to_y, 0),
                (to_down, 0),
            )
        ):
            out[at : at + 48, lo:hi] = value[48 * r : 48 * r + 48]

    for p in range(16):
        slots[48 * p : 48 * p + 48, :] = parts[p][...]
    squares = jnp.zeros((SEL, 128), f32)
    logit = jnp.zeros((SEL, 128), f32)
    for lo in range(0, W, WIDER):
        hi = lo + WIDER
        tile = mm(put[...], slots[:, lo:hi], 1, 0)
        sel[:, lo:hi] = tile.astype(bf16)
        for m in range(0, WIDER, 128):
            lanes = tile[:, m : m + 128]
            squares += lanes * lanes
            logit += lanes * vectors[1:2, lo + m : lo + m + 128]
        scaled[:, lo:hi] = (tile * (vectors[0:1, lo:hi] * DOWN)).astype(bf16)
    squares = jnp.sum(squares, axis=1, keepdims=True)
    logit = jnp.sum(logit, axis=1, keepdims=True)
    write(3 * W, ROW, lanes_of(heads(squares, 3) + heads(logit, 3), SEL))
    for n in range(2):
        for lo in range(0, W, WIDER):
            write(n * W + lo, n * W + lo + WIDER, mm(scaled[...], held[n][:, lo : lo + WIDER], 1, 0))
    for lo in range(W, 2 * W, WIDER):
        gsel[:, lo - W : lo - W + WIDER] = mm(put[...], slots[:, lo : lo + WIDER], 1, 0).astype(
            bf16
        )
    for lo in range(0, W, WIDER):
        write(2 * W + lo, 2 * W + lo + WIDER, mm(gsel[...], held[2][lo : lo + WIDER, :], 1, 1))


def stats(refs):
    tail = 0.0
    for ref in refs:
        tail = tail + ref[:, 3 * W :].astype(f32)
    return (
        tail[:, 0:1] + tail[:, 1:2] + tail[:, 2:3],
        tail[:, 3:4] + tail[:, 4:5] + tail[:, 5:6],
    )


def sum_kernel(keep, from_below, from_above, from_y, to_y, to_far):
    for out, refs in (
        (to_y, (keep.at[48:96], from_below, from_above)),
        (to_far, (keep.at[96:144], from_y)),
    ):
        for k in range(3 * W // TILE):
            cols = slice(k * TILE, (k + 1) * TILE)
            total = refs[0][:, cols].astype(f32)
            for ref in refs[1:]:
                total = total + ref[:, cols].astype(f32)
            out[:, cols] = total.astype(bf16)
        squares, logit = stats(refs)
        out[:, 3 * W :] = lanes_of(heads(squares, 3) + heads(logit, 3), SEL // 8)


def hidden_kernel(keep, near_below, near_above, from_y, from_far, out):
    rows = SEL // 8
    refs = (keep.at[0:48], near_below, near_above, from_y, from_far)

    def total(start):
        value = refs[0][:, start : start + TILE].astype(f32)
        for ref in refs[1:]:
            value = value + ref[:, start : start + TILE].astype(f32)
        return value

    squares, logit = stats(refs)
    scale = lax.rsqrt(squares / D + EPS)
    router_grad = jnp.zeros((rows, 1), f32)
    inner = jnp.zeros((rows, 1), f32)
    for lo in range(0, W, TILE):
        gate = total(lo) * (scale * UP)
        upv = total(W + lo) * (scale * UP)
        back = total(2 * W + lo)
        sigma = jax.nn.sigmoid(gate)
        hidden = (gate * sigma * upv).astype(bf16)
        d_hidden = logit * back
        d_gate = (d_hidden * upv * (sigma + gate * sigma * (1.0 - sigma))).astype(bf16)
        d_up = (d_hidden * gate * sigma).astype(bf16)
        router_grad += jnp.sum(hidden.astype(f32) * back, axis=1, keepdims=True)
        inner += jnp.sum(
            d_gate.astype(f32) * gate + d_up.astype(f32) * upv, axis=1, keepdims=True
        )
        out[:, lo : lo + TILE] = d_gate
        out[:, W + lo : W + lo + TILE] = d_up
        out[:, 2 * W + lo : 2 * W + lo + TILE] = hidden
    out[:, 3 * W :] = lanes_of(
        heads(scale, 3) + heads(logit, 3) + heads(router_grad, 3) + heads(inner, 3), rows
    )


def with_small(rows, small):
    return jnp.concatenate([rows] + heads(small, 2), axis=0).astype(bf16)


def apart(ref):
    value = ref[...].astype(f32)
    n = value.shape[0] - 8
    return value[:n], value[n : n + 4] + value[n + 4 : n + 8]


def to_row(column):
    eye = lax.broadcasted_iota(i32, (SEL, SEL), 0) == lax.broadcasted_iota(i32, (SEL, SEL), 1)
    return jnp.sum(jnp.where(eye, column, 0.0), axis=0, keepdims=True)


def normed_kernel(
    spread, own, above, b2, below, b4, b6, wg, wu, sel, theirs, ours, small, gd, cols
):
    j = pl.program_id(0)

    @pl.when(j == 0)
    def _():
        tail = []
        for r, (ref, at) in enumerate(
            (
                (own, 0),
                (above, 0),
                (b2, 0),
                (below, 0),
                (b4, 0),
                (above, 48),
                (b6, 0),
                (below, 48),
            )
        ):
            gd[48 * r : 48 * r + 48, :] = ref[at : at + 48, 0 : 2 * W]
            tail.append(ref[at : at + 48, 3 * W :].astype(f32))
        tail = jnp.concatenate(tail, axis=0)
        lane = lax.broadcasted_iota(i32, (SEL, 128), 1)

        def value(k):
            return jnp.sum(
                jnp.where((lane >= 3 * k) & (lane < 3 * k + 3), tail, 0.0), axis=1, keepdims=True
            )

        scale, router_grad, inner = value(0), value(2), value(3)
        cols[...] = jnp.where(lane == 0, scale, router_grad)
        small[...] = jnp.zeros(small.shape, f32)
        small[2:3, 0:SEL] = to_row(router_grad)
        small[2:3, SEL : 2 * SEL] = to_row(inner)
        small[3:4, 0:SEL] = to_row(scale)

    part = mm(gd[:, 0:W], wg[...], 1, 1) + mm(gd[:, W : 2 * W], wu[...], 1, 1)
    sel32 = sel[...].astype(f32)
    at = pl.ds(pl.multiple_of(j * W, W), W)
    small[0:1, at] = jnp.sum(part * sel32 * cols[:, 0:1], axis=0, keepdims=True)
    small[1:2, at] = jnp.sum(sel32 * cols[:, 1:2], axis=0, keepdims=True)
    rounded = part.astype(bf16)
    ours[...] = mm(spread[:SEL, :], rounded, 1, 0).astype(bf16)
    theirs[...] = with_small(mm(spread[SEL:, :], rounded, 1, 0), small[0:4, at])


def join_kernel(ours, theirs, mine, up3, down3, far, up1, down1, small):
    rows, other = apart(theirs)
    total = mine[0:4, :] + other
    small[...] = total
    for n, out in ((0, down3), (2, down1), (4, up1), (6, up3), (7, far)):
        at = slice(48 * n, 48 * n + 48)
        out[...] = with_small(ours[at, :].astype(f32) + rows[at], total)


def relay_kernel(
    up2, up2_other, from_below, down2, down2_other, from_above, far, small, to_up, to_down
):
    _, _, _, c = place_of()
    rows, one = apart(far)
    for base, other, ref, mask, out in (
        (up2, up2_other, from_below, c == 0, to_up),
        (down2, down2_other, from_above, c == 1, to_down),
    ):
        chunk, two = apart(ref)
        out[...] = with_small(
            base[...].astype(f32) + other[...].astype(f32) + chunk + jnp.where(mask, rows, 0.0),
            small[...] + two + jnp.where(mask, one, 0.0),
        )


def pair_kernel(stay, stay_other, small, a, b, c, d, here, there):
    total, low = stay[...].astype(f32) + stay_other[...].astype(f32), small[...]
    for part in (a, b, c, d):
        rows, other = apart(part)
        total, low = total + rows, low + other
    here[0:CAP, :] = total[:CAP]
    here[CAP : CAP + 4, :] = low
    there[...] = with_small(total[CAP:], low)


def far_kernel(below, above, _, out):
    out[...] = jnp.where(place_of()[3] == 0, below[...], above[...])


def final_kernel(here, there, mine, go, vectors, sel_row, small, grad_x, d_gain, d_router):
    pick, first, last = pick_of(sel_row[...])
    rows, summed = apart(there)
    own = here[0:CAP, :] + rows
    summed = summed + here[CAP : CAP + 4, :]
    d_gain[...] = summed[0:1]
    d_router[...] = summed[1:2]
    row = compact_of(lax.broadcasted_iota(i32, (1, SEL), 1))
    k = lax.broadcasted_iota(i32, (CAP, SEL), 0)
    where = (row == first + k) & (row < last)

    def place(values):
        return jnp.sum(jnp.where(where, values, 0.0), axis=1, keepdims=True)

    scale = place(small[3:4, 0:SEL])
    router_grad = place(summed[2:3, 0:SEL])
    inner = place(summed[2:3, SEL : 2 * SEL])
    d_sel = (
        scale * vectors[0:1, :] * own
        - mine[:, 0:W].astype(f32) * (scale * scale * inner / D)
        + router_grad * vectors[1:2, :]
    )
    spread = jnp.zeros((TOK, W), f32)
    for piece in heads(d_sel, 3):
        spread += mm(pick, piece.astype(bf16), 1, 0)
    grad_x[...] = (go[...].astype(f32) + spread).astype(bf16)


def gather(pair, after):
    held = {0: pair}
    for k in (2, 1):
        held[-k] = along(pair, k)
        held[k] = along(pair, -k)
    held[-3] = along(held[-2], 1)
    held[3] = along(held[2], -1)
    far = pl.pallas_call(
        far_kernel,
        out_shape=jax.ShapeDtypeStruct(pair.shape, bf16),
        in_specs=[VMEM] * 2 + [pl.BlockSpec(memory_space=pl.ANY)],
        out_specs=VMEM,
        compiler_params=params(16),
        name="far",
    )(held[-2], held[2], after)
    held[4] = lax.ppermute(far, "wide", ZFAR)
    ours = [held[k] for k in range(-3, 5)]
    return ours + [lax.ppermute(piece, "wide", CORE) for piece in ours]


def local(tokens, grad_out, selected, gain, router_weight, w_gate, w_up, w_down):
    sel_col = selected.reshape(SEL, 1)
    gain = gain.reshape(1, W)
    router_weight = router_weight.reshape(1, W)
    anywhere = pl.BlockSpec(memory_space=pl.ANY)
    mine, sel_row = pl.pallas_call(
        own_kernel,
        out_shape=(
            jax.ShapeDtypeStruct((CAP, 2 * W), bf16),
            jax.ShapeDtypeStruct((1, SEL), i32),
        ),
        in_specs=[anywhere] * 3,
        out_specs=(VMEM, VMEM),
        scratch_shapes=[pltpu.VMEM((SEL,), i32)]
        + [pltpu.VMEM((TOK, W), bf16)] * 2
        + [pltpu.SemaphoreType.DMA((3,))],
        compiler_params=params(60),
        name="own",
    )(selected, tokens, grad_out)
    put, spread, vectors, *weights = pl.pallas_call(
        onehot_kernel,
        out_shape=(
            jax.ShapeDtypeStruct((SEL, 2 * SEL), bf16),
            jax.ShapeDtypeStruct((2 * SEL, SEL), bf16),
            jax.ShapeDtypeStruct((2, W), f32),
        )
        + (jax.ShapeDtypeStruct((W, W), bf16),) * 3,
        in_specs=[VMEM] * 3 + [anywhere] * 4,
        out_specs=(VMEM,) * 6,
        scratch_shapes=[pltpu.SemaphoreType.DMA((3,))],
        compiler_params=params(16),
        name="onehot",
    )(sel_col, gain, router_weight, mine, w_gate, w_up, w_down)
    pair = jnp.concatenate([mine, lax.ppermute(mine, "wide", YLO)], axis=0)
    parts = gather(pair, put)

    full = lambda *shape: pl.BlockSpec(shape, lambda j: (0,) * len(shape))
    block = jax.ShapeDtypeStruct((48, ROW), bf16)
    sel, gsel, keep, to_up, to_down, to_y, *near = pl.pallas_call(
        forward_kernel,
        out_shape=(
            jax.ShapeDtypeStruct((SEL, W), bf16),
            jax.ShapeDtypeStruct((SEL, W), bf16),
            jax.ShapeDtypeStruct((144, ROW), bf16),
        )
        + (block,) * 5,
        in_specs=[VMEM] * 21,
        out_specs=(VMEM,) * 8,
        scratch_shapes=[pltpu.VMEM((768, 2 * W), bf16), pltpu.VMEM((SEL, W), bf16)],
        compiler_params=params(16),
        cost_estimate=cost(3.6e9, 16e6),
        name="forward",
    )(*parts, put, vectors, *weights)

    from_below = lax.ppermute(to_up, "narrow", XUP)
    from_above = lax.ppermute(to_down, "narrow", XDOWN)
    from_y = lax.ppermute(to_y, "narrow", YHI)
    near = lax.ppermute(near[0], "narrow", XUP), lax.ppermute(near[1], "narrow", XDOWN)
    to_y, to_far = pl.pallas_call(
        sum_kernel,
        out_shape=(block, block),
        in_specs=[VMEM] * 4,
        out_specs=(VMEM, VMEM),
        compiler_params=params(8),
        name="sum",
    )(keep, from_below, from_above, from_y)
    from_far = lax.ppermute(to_far, "narrow", XFAR)
    from_y = lax.ppermute(to_y, "narrow", YHI)
    own = pl.pallas_call(
        hidden_kernel,
        out_shape=block,
        in_specs=[VMEM] * 5,
        out_specs=VMEM,
        compiler_params=params(8),
        name="hidden",
    )(keep, *near, from_y, from_far)

    b2 = lax.ppermute(own, "narrow", XFAR)
    b4 = lax.ppermute(own, "narrow", YHI)
    column = jnp.concatenate([own, b4], axis=0)
    below = lax.ppermute(column, "narrow", XUP)
    above = lax.ppermute(column, "narrow", XDOWN)
    b6 = lax.ppermute(b2, "narrow", YHI)

    theirs, ours, small = pl.pallas_call(
        normed_kernel,
        grid=(W // W,),
        out_shape=(
            jax.ShapeDtypeStruct((SEL + 8, W), bf16),
            jax.ShapeDtypeStruct((SEL, W), bf16),
            jax.ShapeDtypeStruct((8, W), f32),
        ),
        in_specs=[VMEM] * 7
        + [pl.BlockSpec((W, W), lambda j: (j, 0))] * 2
        + [pl.BlockSpec((SEL, W), lambda j: (0, j))],
        out_specs=(
            pl.BlockSpec((SEL + 8, W), lambda j: (0, j)),
            pl.BlockSpec((SEL, W), lambda j: (0, j)),
            full(8, W),
        ),
        scratch_shapes=[pltpu.VMEM((SEL, 2 * W), bf16), pltpu.VMEM((SEL, 128), f32)],
        compiler_params=params(),
        cost_estimate=cost(2.4e9, 9e6),
        name="normed",
    )(spread, own, above, b2, below, b4, b6, w_gate, w_up, sel)

    part = jax.ShapeDtypeStruct((56, W), bf16)
    theirs = lax.ppermute(theirs, "wide", CORE)
    up3, down3, far, up1, down1, total = pl.pallas_call(
        join_kernel,
        out_shape=(part,) * 5 + (jax.ShapeDtypeStruct((4, W), f32),),
        in_specs=[VMEM] * 3,
        out_specs=(VMEM,) * 6,
        compiler_params=params(16),
        name="join",
    )(ours, theirs, small)
    from_below, from_above = along(up3, 1), along(down3, -1)
    far = lax.ppermute(far, "wide", ZFAR)
    near = along(up1, 1), along(down1, -1)

    def chunk(n):
        return pl.BlockSpec((48, W), lambda j: (n, 0))

    up2, down2 = pl.pallas_call(
        relay_kernel,
        grid=(1,),
        out_shape=(part, part),
        in_specs=[chunk(5), chunk(5), full(56, W), chunk(1), chunk(1)]
        + [full(56, W), full(56, W), full(4, W)],
        out_specs=(full(56, W), full(56, W)),
        compiler_params=params(16),
        name="relay",
    )(ours, theirs, from_below, ours, theirs, from_above, far, total)
    here, there = pl.pallas_call(
        pair_kernel,
        grid=(1,),
        out_shape=(
            jax.ShapeDtypeStruct((CAP + 4, W), f32),
            jax.ShapeDtypeStruct((CAP + 8, W), bf16),
        ),
        in_specs=[chunk(3), chunk(3), full(4, W)] + [full(56, W)] * 4,
        out_specs=(full(CAP + 4, W), full(CAP + 8, W)),
        compiler_params=params(16),
        name="pair",
    )(ours, theirs, total, *near, along(up2, 2), along(down2, -2))
    there = lax.ppermute(there, "wide", YLO)

    rows = jnp.concatenate([own, above[:48], b2, below[:48], b4, above[48:], b6, below[48:]])
    tail = rows[:, 3 * W :].astype(f32)
    scale = jnp.sum(tail[:, 0:3], axis=1, keepdims=True)
    logit = jnp.sum(tail[:, 3:6], axis=1, keepdims=True)
    normed = (sel.astype(f32) * scale * gain).astype(bf16)
    d_out = (logit * gsel.astype(f32)).astype(bf16)
    grad_gate = mm(normed, rows[:, :W], 0, 0).astype(bf16)
    grad_up = mm(normed, rows[:, W : 2 * W], 0, 0).astype(bf16)
    grad_down = mm(rows[:, 2 * W : 3 * W], d_out, 0, 0).astype(bf16)

    vector = jax.ShapeDtypeStruct((1, W), f32)
    grad_x, d_gain, d_router = pl.pallas_call(
        final_kernel,
        out_shape=(jax.ShapeDtypeStruct((TOK, W), bf16), vector, vector),
        in_specs=[VMEM] * 7,
        out_specs=(VMEM,) * 3,
        compiler_params=params(16),
        name="final",
    )(here, there, mine, grad_out, vectors, sel_row, small)
    return (grad_x, grad_gate, grad_up, grad_down, d_gain.reshape(W), d_router.reshape(W))


def solution(mesh):
    return jax.shard_map(
        local,
        mesh=mesh,
        in_specs=(
            P("wide", "narrow"),
            P("wide", "narrow"),
            P(),
            P("narrow"),
            P("narrow"),
            P("narrow", "wide"),
            P("narrow", "wide"),
            P("wide", "narrow"),
        ),
        out_specs=(
            P("wide", "narrow"),
            P("narrow", "wide"),
            P("narrow", "wide"),
            P("wide", "narrow"),
            P("narrow"),
            P("narrow"),
        ),
        check_vma=False,
    )
```

```python
import jax
import jax.numpy as jnp
from jax import lax
from jax.experimental import pallas as pl
from jax.experimental.pallas import tpu as pltpu
from jax.sharding import PartitionSpec as P

D = 8192
EPS = 1e-06
bf16 = jnp.bfloat16
f32 = jnp.float32
i32 = jnp.int32
DOWN, UP = 2.0**-20, 2.0**20
TOK = 96
CAP = 24
SEL = 384
W = 1024
TILE = 256
WIDER = 512

WIDE = [(z, y, c) for z in range(8) for y in range(2) for c in range(2)]


def wide_pairs(move):
    def index(z, y, c):
        return (z % 8 * 2 + y) * 2 + c

    return [(index(*t), index(*move(*t))) for t in WIDE]


CORE = wide_pairs(lambda z, y, c: (z, y, 1 - c))
YLO = wide_pairs(lambda z, y, c: (z, 1 - y, c))
XUP = [(n, n // 4 * 4 + (n + 1) % 4) for n in range(8)]
XDOWN = [(n, n // 4 * 4 + (n + 3) % 4) for n in range(8)]
XFAR = [(n, n // 4 * 4 + (n + 2) % 4) for n in range(8)]
YHI = [(n, (n + 4) % 8) for n in range(8)]
ROW = 3 * 1024 + 128
ZFAR = wide_pairs(lambda z, y, c: (z + 2 + 4 * c, y, c))


def along(value, step):
    return lax.ppermute(value, "wide", wide_pairs(lambda z, y, c: (z + 8 + step, y, c)))


VMEM = pl.BlockSpec(memory_space=pltpu.VMEM)


def params(mib=24):
    return pltpu.CompilerParams(vmem_limit_bytes=mib << 20)


def cost(flops, bytes_):
    return pl.CostEstimate(flops=int(flops), bytes_accessed=int(bytes_), transcendentals=0)


def heads(value, count):
    out = []
    for _ in range(count):
        head = value.astype(bf16).astype(f32)
        out.append(head)
        value = jnp.where(jnp.abs(head) < jnp.inf, value - head, 0.0)
    return out


def lanes_of(columns, rows):
    lane = lax.broadcasted_iota(i32, (rows, 128), 1)
    out = jnp.zeros((rows, 128), f32)
    for k, column in enumerate(columns):
        out = jnp.where(lane == k, column, out)
    return out.astype(bf16)


def span(i, size, start=0):
    return pl.ds(pl.multiple_of(start + i * size, size), size)


def mm(a, b, ca, cb):
    return lax.dot_general(a, b, (((ca,), (cb,)), ((), ())), preferred_element_type=f32)


def place_of():
    w = lax.axis_index("wide")
    return w, w // 4, (w // 2) % 2, w % 2


def count_before(sel_col, ids):
    return jnp.sum(jnp.where(sel_col < ids, 1, 0).astype(i32), axis=0, keepdims=True)


def compact_of(i):
    n = lax.axis_index("narrow")
    r = (i * 1366) >> 16
    block = (r & 4 ^ n & 4) | ((r + n) & 3)
    return i + (block - r) * 48


def placement(sel_col, begin, size):
    _, z, y, c = place_of()
    slot = begin + lax.broadcasted_iota(i32, (1, size), 1)
    n = (slot * 2731) >> 16
    k = slot - n * CAP
    zz = (z + ((n >> 1) & 7) + 5) & 7
    block = zz * 4 + (y ^ (n & 1)) * 2 + (c ^ (n >> 4))
    start = count_before(sel_col, block * TOK)
    end = count_before(sel_col, block * TOK + TOK)
    row = compact_of(lax.broadcasted_iota(i32, (SEL, 1), 0))
    return jnp.where((row == start + k) & (row < end), 1.0, 0.0)


def pick_of(sel_row):
    w, _, _, _ = place_of()

    def before(ids):
        return jnp.sum(jnp.where(sel_row < ids, 1, 0).astype(i32), axis=1, keepdims=True)

    ids = w * TOK + lax.broadcasted_iota(i32, (TOK, 1), 0)
    first = before(jnp.full((1, 1), w * TOK, i32))
    last = before(jnp.full((1, 1), w * TOK + TOK, i32))
    rank = before(ids) - first
    marked = before(ids + 1) - before(ids) > 0
    k = lax.broadcasted_iota(i32, (TOK, CAP), 1)
    return jnp.where((k == rank) & marked, 1.0, 0.0).astype(bf16), first, last


def own_kernel(sel_hbm, tok_hbm, go_hbm, out, row, sel, tok, go, sems):
    copies = [
        pltpu.make_async_copy(tok_hbm, tok, sems.at[0]),
        pltpu.make_async_copy(go_hbm, go, sems.at[1]),
        pltpu.make_async_copy(sel_hbm, sel, sems.at[2]),
    ]
    for copy in copies:
        copy.start()
    copies[2].wait()
    sel_row = sel[...].reshape(1, SEL)
    row[...] = sel_row
    pick = pick_of(sel_row)[0]
    for n, held in enumerate((tok, go)):
        copies[n].wait()
        out[:, n * W : n * W + W] = mm(pick, held[...], 0, 0).astype(bf16)


def onehot_kernel(sel_col, gain, rw, _, *refs):
    weights, (put, spread, vectors), held, sems = refs[:3], refs[3:6], refs[6:9], refs[9]
    loads = [pltpu.make_async_copy(weights[n], held[n], sems.at[n]) for n in range(3)]
    for load in loads:
        load.start()
    vectors[0:1, :] = gain[...]
    vectors[1:2, :] = rw[...]
    @pl.loop(0, 2 * SEL // 128)
    def _(i):
        hot = placement(sel_col[...], i * 128, 128)
        put[:, span(i, 128)] = hot.astype(bf16)
        spread[span(i, 128), :] = hot.T.astype(bf16)

    for load in loads:
        load.wait()


def forward_kernel(*refs):
    parts = refs[:16]
    put, vectors, *held, sel, gsel, keep = refs[16:24]
    to_up, to_down, to_y, near_up, near_down, slots, scaled = refs[24:]

    def write(lo, hi, value):
        value = value.astype(bf16)
        for r, (out, at) in enumerate(
            (
                (keep, 0),
                (near_up, 0),
                (keep, 96),
                (near_down, 0),
                (keep, 48),
                (to_up, 0),
                (to_y, 0),
                (to_down, 0),
            )
        ):
            out[at : at + 48, lo:hi] = value[48 * r : 48 * r + 48]

    for p in range(16):
        slots[48 * p : 48 * p + 48, :] = parts[p][...]
    squares = jnp.zeros((SEL, 128), f32)
    logit = jnp.zeros((SEL, 128), f32)
    for lo in range(0, W, WIDER):
        hi = lo + WIDER
        tile = mm(put[...], slots[:, lo:hi], 1, 0)
        sel[:, lo:hi] = tile.astype(bf16)
        for m in range(0, WIDER, 128):
            lanes = tile[:, m : m + 128]
            squares += lanes * lanes
            logit += lanes * vectors[1:2, lo + m : lo + m + 128]
        scaled[:, lo:hi] = (tile * (vectors[0:1, lo:hi] * DOWN)).astype(bf16)
    squares = jnp.sum(squares, axis=1, keepdims=True)
    logit = jnp.sum(logit, axis=1, keepdims=True)
    write(3 * W, ROW, lanes_of(heads(squares, 3) + heads(logit, 3), SEL))
    for n in range(2):
        for lo in range(0, W, WIDER):
            write(n * W + lo, n * W + lo + WIDER, mm(scaled[...], held[n][:, lo : lo + WIDER], 1, 0))
    for lo in range(W, 2 * W, WIDER):
        gsel[:, lo - W : lo - W + WIDER] = mm(put[...], slots[:, lo : lo + WIDER], 1, 0).astype(
            bf16
        )
    for lo in range(0, W, WIDER):
        write(2 * W + lo, 2 * W + lo + WIDER, mm(gsel[...], held[2][lo : lo + WIDER, :], 1, 1))


def stats(refs):
    tail = 0.0
    for ref in refs:
        tail = tail + ref[:, 3 * W :].astype(f32)
    return (
        tail[:, 0:1] + tail[:, 1:2] + tail[:, 2:3],
        tail[:, 3:4] + tail[:, 4:5] + tail[:, 5:6],
    )


def sum_kernel(keep, from_below, from_above, from_y, to_y, to_far):
    for out, refs in (
        (to_y, (keep.at[48:96], from_below, from_above)),
        (to_far, (keep.at[96:144], from_y)),
    ):

        @pl.loop(0, 3 * W // TILE)
        def _(k, out=out, refs=refs):
            cols = span(k, TILE)
            total = refs[0][:, cols].astype(f32)
            for ref in refs[1:]:
                total = total + ref[:, cols].astype(f32)
            out[:, cols] = total.astype(bf16)

        squares, logit = stats(refs)
        out[:, 3 * W :] = lanes_of(heads(squares, 3) + heads(logit, 3), SEL // 8)


def hidden_kernel(keep, near_below, near_above, from_y, from_far, out):
    rows = SEL // 8
    refs = (keep.at[0:48], near_below, near_above, from_y, from_far)

    squares, logit = stats(refs)
    scale = lax.rsqrt(squares / D + EPS)

    def tile(i, carry):
        router_grad, inner = carry

        def total(start):
            cols = span(i, TILE, start)
            value = refs[0][:, cols].astype(f32)
            for ref in refs[1:]:
                value = value + ref[:, cols].astype(f32)
            return value

        gate = total(0) * (scale * UP)
        upv = total(W) * (scale * UP)
        back = total(2 * W)
        sigma = jax.nn.sigmoid(gate)
        hidden = (gate * sigma * upv).astype(bf16)
        d_hidden = logit * back
        d_gate = (d_hidden * upv * (sigma + gate * sigma * (1.0 - sigma))).astype(bf16)
        d_up = (d_hidden * gate * sigma).astype(bf16)
        router_grad += jnp.sum(hidden.astype(f32) * back, axis=1, keepdims=True)
        inner += jnp.sum(
            d_gate.astype(f32) * gate + d_up.astype(f32) * upv, axis=1, keepdims=True
        )
        out[:, span(i, TILE)] = d_gate
        out[:, span(i, TILE, W)] = d_up
        out[:, span(i, TILE, 2 * W)] = hidden
        return router_grad, inner

    zero = jnp.zeros((rows, 1), f32)
    router_grad, inner = lax.fori_loop(0, W // TILE, tile, (zero, zero))
    out[:, 3 * W :] = lanes_of(
        heads(scale, 3) + heads(logit, 3) + heads(router_grad, 3) + heads(inner, 3), rows
    )


def with_small(rows, small):
    return jnp.concatenate([rows] + heads(small, 2), axis=0).astype(bf16)


def apart(ref, cols):
    value = ref[:, cols].astype(f32)
    n = value.shape[0] - 8
    return value[:n], value[n : n + 4] + value[n + 4 : n + 8]


def to_row(column):
    eye = lax.broadcasted_iota(i32, (SEL, SEL), 0) == lax.broadcasted_iota(i32, (SEL, SEL), 1)
    return jnp.sum(jnp.where(eye, column, 0.0), axis=0, keepdims=True)


def normed_kernel(
    spread, own, above, b2, below, b4, b6, wg, wu, sel, theirs, ours, small, gd, cols
):
    j = pl.program_id(0)

    @pl.when(j == 0)
    def _():
        tail = []
        for r, (ref, at) in enumerate(
            (
                (own, 0),
                (above, 0),
                (b2, 0),
                (below, 0),
                (b4, 0),
                (above, 48),
                (b6, 0),
                (below, 48),
            )
        ):
            gd[48 * r : 48 * r + 48, :] = ref[at : at + 48, 0 : 2 * W]
            tail.append(ref[at : at + 48, 3 * W :].astype(f32))
        tail = jnp.concatenate(tail, axis=0)
        lane = lax.broadcasted_iota(i32, (SEL, 128), 1)

        def value(k):
            return jnp.sum(
                jnp.where((lane >= 3 * k) & (lane < 3 * k + 3), tail, 0.0), axis=1, keepdims=True
            )

        scale, router_grad, inner = value(0), value(2), value(3)
        cols[...] = jnp.where(lane == 0, scale, router_grad)
        small[...] = jnp.zeros(small.shape, f32)
        small[2:3, 0:SEL] = to_row(router_grad)
        small[2:3, SEL : 2 * SEL] = to_row(inner)
        small[3:4, 0:SEL] = to_row(scale)

    part = mm(gd[:, 0:W], wg[...], 1, 1) + mm(gd[:, W : 2 * W], wu[...], 1, 1)
    sel32 = sel[...].astype(f32)
    at = pl.ds(pl.multiple_of(j * W, W), W)
    small[0:1, at] = jnp.sum(part * sel32 * cols[:, 0:1], axis=0, keepdims=True)
    small[1:2, at] = jnp.sum(sel32 * cols[:, 1:2], axis=0, keepdims=True)
    rounded = part.astype(bf16)
    ours[...] = mm(spread[:SEL, :], rounded, 1, 0).astype(bf16)
    theirs[...] = with_small(mm(spread[SEL:, :], rounded, 1, 0), small[0:4, at])


def join_kernel(ours, theirs, mine, up3, down3, far, up1, down1, small):
    @pl.loop(0, W // TILE)
    def _(i):
        cols = span(i, TILE)
        rows, other = apart(theirs, cols)
        total = mine[0:4, cols] + other
        small[:, cols] = total
        for n, out in ((0, down3), (2, down1), (4, up1), (6, up3), (7, far)):
            at = slice(48 * n, 48 * n + 48)
            out[:, cols] = with_small(ours[at, cols].astype(f32) + rows[at], total)


def relay_kernel(
    up2, up2_other, from_below, down2, down2_other, from_above, far, small, to_up, to_down
):
    _, _, _, c = place_of()

    @pl.loop(0, W // TILE)
    def _(i):
        cols = span(i, TILE)
        rows, one = apart(far, cols)
        for base, other, ref, mask, out in (
            (up2, up2_other, from_below, c == 0, to_up),
            (down2, down2_other, from_above, c == 1, to_down),
        ):
            chunk, two = apart(ref, cols)
            chunk += base[:, cols].astype(f32) + other[:, cols].astype(f32)
            out[:, cols] = with_small(
                chunk + jnp.where(mask, rows, 0.0),
                small[:, cols] + two + jnp.where(mask, one, 0.0),
            )


def pair_kernel(stay, stay_other, small, a, b, c, d, here, there):
    @pl.loop(0, W // TILE)
    def _(i):
        cols = span(i, TILE)
        total = stay[:, cols].astype(f32) + stay_other[:, cols].astype(f32)
        low = small[:, cols]
        for part in (a, b, c, d):
            rows, other = apart(part, cols)
            total, low = total + rows, low + other
        here[0:CAP, cols] = total[:CAP]
        here[CAP : CAP + 4, cols] = low
        there[:, cols] = with_small(total[CAP:], low)


def far_kernel(below, above, _, out):
    out[...] = jnp.where(place_of()[3] == 0, below[...], above[...])


def final_kernel(
    here, there, mine, go, vectors, sel_row, small, grad_x, d_gain, d_router, held
):
    pick, first, last = pick_of(sel_row[...])
    own, summed = apart(there, slice(0, W))
    own = own + here[0:CAP, :]
    summed = summed + here[CAP : CAP + 4, :]
    d_gain[...] = summed[0:1]
    d_router[...] = summed[1:2]
    row = compact_of(lax.broadcasted_iota(i32, (1, SEL), 1))
    k = lax.broadcasted_iota(i32, (CAP, SEL), 0)
    where = (row == first + k) & (row < last)

    def place(values):
        return jnp.sum(jnp.where(where, values, 0.0), axis=1, keepdims=True)

    scale = place(small[3:4, 0:SEL])
    router_grad = place(summed[2:3, 0:SEL])
    inner = place(summed[2:3, SEL : 2 * SEL])
    held[...] = own

    @pl.loop(0, W // TILE)
    def _(i):
        cols = span(i, TILE)
        d_sel = (
            scale * vectors[0:1, cols] * held[:, cols]
            - mine[:, cols].astype(f32) * (scale * scale * inner / D)
            + router_grad * vectors[1:2, cols]
        )
        spread = jnp.zeros((TOK, TILE), f32)
        for piece in heads(d_sel, 3):
            spread += mm(pick, piece.astype(bf16), 1, 0)
        grad_x[:, cols] = (go[:, cols].astype(f32) + spread).astype(bf16)


def gather(pair, after):
    held = {0: pair}
    for k in (2, 1):
        held[-k] = along(pair, k)
        held[k] = along(pair, -k)
    held[-3] = along(held[-2], 1)
    held[3] = along(held[2], -1)
    far = pl.pallas_call(
        far_kernel,
        out_shape=jax.ShapeDtypeStruct(pair.shape, bf16),
        in_specs=[VMEM] * 2 + [pl.BlockSpec(memory_space=pl.ANY)],
        out_specs=VMEM,
        compiler_params=params(16),
        name="far",
    )(held[-2], held[2], after)
    held[4] = lax.ppermute(far, "wide", ZFAR)
    ours = [held[k] for k in range(-3, 5)]
    return ours + [lax.ppermute(piece, "wide", CORE) for piece in ours]


def local(tokens, grad_out, selected, gain, router_weight, w_gate, w_up, w_down):
    sel_col = selected.reshape(SEL, 1)
    gain = gain.reshape(1, W)
    router_weight = router_weight.reshape(1, W)
    anywhere = pl.BlockSpec(memory_space=pl.ANY)
    mine, sel_row = pl.pallas_call(
        own_kernel,
        out_shape=(
            jax.ShapeDtypeStruct((CAP, 2 * W), bf16),
            jax.ShapeDtypeStruct((1, SEL), i32),
        ),
        in_specs=[anywhere] * 3,
        out_specs=(VMEM, VMEM),
        scratch_shapes=[pltpu.VMEM((SEL,), i32)]
        + [pltpu.VMEM((TOK, W), bf16)] * 2
        + [pltpu.SemaphoreType.DMA((3,))],
        compiler_params=params(60),
        name="own",
    )(selected, tokens, grad_out)
    put, spread, vectors, *weights = pl.pallas_call(
        onehot_kernel,
        out_shape=(
            jax.ShapeDtypeStruct((SEL, 2 * SEL), bf16),
            jax.ShapeDtypeStruct((2 * SEL, SEL), bf16),
            jax.ShapeDtypeStruct((2, W), f32),
        )
        + (jax.ShapeDtypeStruct((W, W), bf16),) * 3,
        in_specs=[VMEM] * 3 + [anywhere] * 4,
        out_specs=(VMEM,) * 6,
        scratch_shapes=[pltpu.SemaphoreType.DMA((3,))],
        compiler_params=params(16),
        name="onehot",
    )(sel_col, gain, router_weight, mine, w_gate, w_up, w_down)
    pair = jnp.concatenate([mine, lax.ppermute(mine, "wide", YLO)], axis=0)
    parts = gather(pair, put)

    full = lambda *shape: pl.BlockSpec(shape, lambda j: (0,) * len(shape))
    block = jax.ShapeDtypeStruct((48, ROW), bf16)
    sel, gsel, keep, to_up, to_down, to_y, *near = pl.pallas_call(
        forward_kernel,
        out_shape=(
            jax.ShapeDtypeStruct((SEL, W), bf16),
            jax.ShapeDtypeStruct((SEL, W), bf16),
            jax.ShapeDtypeStruct((144, ROW), bf16),
        )
        + (block,) * 5,
        in_specs=[VMEM] * 21,
        out_specs=(VMEM,) * 8,
        scratch_shapes=[pltpu.VMEM((768, 2 * W), bf16), pltpu.VMEM((SEL, W), bf16)],
        compiler_params=params(16),
        cost_estimate=cost(3.6e9, 16e6),
        name="forward",
    )(*parts, put, vectors, *weights)

    from_below = lax.ppermute(to_up, "narrow", XUP)
    from_above = lax.ppermute(to_down, "narrow", XDOWN)
    from_y = lax.ppermute(to_y, "narrow", YHI)
    near = lax.ppermute(near[0], "narrow", XUP), lax.ppermute(near[1], "narrow", XDOWN)
    to_y, to_far = pl.pallas_call(
        sum_kernel,
        out_shape=(block, block),
        in_specs=[VMEM] * 4,
        out_specs=(VMEM, VMEM),
        compiler_params=params(8),
        name="sum",
    )(keep, from_below, from_above, from_y)
    from_far = lax.ppermute(to_far, "narrow", XFAR)
    from_y = lax.ppermute(to_y, "narrow", YHI)
    own = pl.pallas_call(
        hidden_kernel,
        out_shape=block,
        in_specs=[VMEM] * 5,
        out_specs=VMEM,
        compiler_params=params(8),
        name="hidden",
    )(keep, *near, from_y, from_far)

    b2 = lax.ppermute(own, "narrow", XFAR)
    b4 = lax.ppermute(own, "narrow", YHI)
    column = jnp.concatenate([own, b4], axis=0)
    below = lax.ppermute(column, "narrow", XUP)
    above = lax.ppermute(column, "narrow", XDOWN)
    b6 = lax.ppermute(b2, "narrow", YHI)

    theirs, ours, small = pl.pallas_call(
        normed_kernel,
        grid=(W // W,),
        out_shape=(
            jax.ShapeDtypeStruct((SEL + 8, W), bf16),
            jax.ShapeDtypeStruct((SEL, W), bf16),
            jax.ShapeDtypeStruct((8, W), f32),
        ),
        in_specs=[VMEM] * 7
        + [pl.BlockSpec((W, W), lambda j: (j, 0))] * 2
        + [pl.BlockSpec((SEL, W), lambda j: (0, j))],
        out_specs=(
            pl.BlockSpec((SEL + 8, W), lambda j: (0, j)),
            pl.BlockSpec((SEL, W), lambda j: (0, j)),
            full(8, W),
        ),
        scratch_shapes=[pltpu.VMEM((SEL, 2 * W), bf16), pltpu.VMEM((SEL, 128), f32)],
        compiler_params=params(),
        cost_estimate=cost(2.4e9, 9e6),
        name="normed",
    )(spread, own, above, b2, below, b4, b6, w_gate, w_up, sel)

    part = jax.ShapeDtypeStruct((56, W), bf16)
    theirs = lax.ppermute(theirs, "wide", CORE)
    up3, down3, far, up1, down1, total = pl.pallas_call(
        join_kernel,
        out_shape=(part,) * 5 + (jax.ShapeDtypeStruct((4, W), f32),),
        in_specs=[VMEM] * 3,
        out_specs=(VMEM,) * 6,
        compiler_params=params(16),
        name="join",
    )(ours, theirs, small)
    from_below, from_above = along(up3, 1), along(down3, -1)
    far = lax.ppermute(far, "wide", ZFAR)
    near = along(up1, 1), along(down1, -1)

    def chunk(n):
        return pl.BlockSpec((48, W), lambda j: (n, 0))

    up2, down2 = pl.pallas_call(
        relay_kernel,
        grid=(1,),
        out_shape=(part, part),
        in_specs=[chunk(5), chunk(5), full(56, W), chunk(1), chunk(1)]
        + [full(56, W), full(56, W), full(4, W)],
        out_specs=(full(56, W), full(56, W)),
        compiler_params=params(16),
        name="relay",
    )(ours, theirs, from_below, ours, theirs, from_above, far, total)
    here, there = pl.pallas_call(
        pair_kernel,
        grid=(1,),
        out_shape=(
            jax.ShapeDtypeStruct((CAP + 4, W), f32),
            jax.ShapeDtypeStruct((CAP + 8, W), bf16),
        ),
        in_specs=[chunk(3), chunk(3), full(4, W)] + [full(56, W)] * 4,
        out_specs=(full(CAP + 4, W), full(CAP + 8, W)),
        compiler_params=params(16),
        name="pair",
    )(ours, theirs, total, *near, along(up2, 2), along(down2, -2))
    there = lax.ppermute(there, "wide", YLO)

    rows = jnp.concatenate([own, above[:48], b2, below[:48], b4, above[48:], b6, below[48:]])
    tail = rows[:, 3 * W :].astype(f32)
    scale = jnp.sum(tail[:, 0:3], axis=1, keepdims=True)
    logit = jnp.sum(tail[:, 3:6], axis=1, keepdims=True)
    normed = (sel.astype(f32) * scale * gain).astype(bf16)
    d_out = (logit * gsel.astype(f32)).astype(bf16)
    grad_gate = mm(normed, rows[:, :W], 0, 0).astype(bf16)
    grad_up = mm(normed, rows[:, W : 2 * W], 0, 0).astype(bf16)
    grad_down = mm(rows[:, 2 * W : 3 * W], d_out, 0, 0).astype(bf16)

    vector = jax.ShapeDtypeStruct((1, W), f32)
    grad_x, d_gain, d_router = pl.pallas_call(
        final_kernel,
        out_shape=(jax.ShapeDtypeStruct((TOK, W), bf16), vector, vector),
        in_specs=[VMEM] * 7,
        out_specs=(VMEM,) * 3,
        scratch_shapes=[pltpu.VMEM((CAP, W), f32)],
        compiler_params=params(16),
        name="final",
    )(here, there, mine, grad_out, vectors, sel_row, small)
    return (grad_x, grad_gate, grad_up, grad_down, d_gain.reshape(W), d_router.reshape(W))


def solution(mesh):
    return jax.shard_map(
        local,
        mesh=mesh,
        in_specs=(
            P("wide", "narrow"),
            P("wide", "narrow"),
            P(),
            P("narrow"),
            P("narrow"),
            P("narrow", "wide"),
            P("narrow", "wide"),
            P("wide", "narrow"),
        ),
        out_specs=(
            P("wide", "narrow"),
            P("narrow", "wide"),
            P("narrow", "wide"),
            P("wide", "narrow"),
            P("narrow"),
            P("narrow"),
        ),
        check_vma=False,
    )
```

```python
import jax
import jax.numpy as jnp
from jax import lax
from jax.experimental import pallas as pl
from jax.experimental.pallas import tpu as pltpu
from jax.sharding import PartitionSpec as P

D = 8192
EPS = 1e-06
bf16 = jnp.bfloat16
f32 = jnp.float32
i32 = jnp.int32
DOWN, UP = 2.0**-20, 2.0**20
TOK = 96
CAP = 24
SEL = 384
W = 1024
TILE = 256
WIDER = 512

WIDE = [(z, y, c) for z in range(8) for y in range(2) for c in range(2)]


def wide_pairs(move):
    def index(z, y, c):
        return (z % 8 * 2 + y) * 2 + c

    return [(index(*t), index(*move(*t))) for t in WIDE]


CORE = wide_pairs(lambda z, y, c: (z, y, 1 - c))
YLO = wide_pairs(lambda z, y, c: (z, 1 - y, c))
XUP = [(n, n // 4 * 4 + (n + 1) % 4) for n in range(8)]
XDOWN = [(n, n // 4 * 4 + (n + 3) % 4) for n in range(8)]
XFAR = [(n, n // 4 * 4 + (n + 2) % 4) for n in range(8)]
YHI = [(n, (n + 4) % 8) for n in range(8)]
ROW = 3 * 1024 + 128
ZFAR = wide_pairs(lambda z, y, c: (z + 2 + 4 * c, y, c))


def along(value, step):
    return lax.ppermute(value, "wide", wide_pairs(lambda z, y, c: (z + 8 + step, y, c)))


VMEM = pl.BlockSpec(memory_space=pltpu.VMEM)


def params(mib=24):
    return pltpu.CompilerParams(vmem_limit_bytes=mib << 20)


def cost(flops, bytes_):
    return pl.CostEstimate(flops=int(flops), bytes_accessed=int(bytes_), transcendentals=0)


def heads(value, count):
    out = []
    for _ in range(count):
        head = value.astype(bf16).astype(f32)
        out.append(head)
        value = jnp.where(jnp.abs(head) < jnp.inf, value - head, 0.0)
    return out


def lanes_of(columns, rows):
    lane = lax.broadcasted_iota(i32, (rows, 128), 1)
    out = jnp.zeros((rows, 128), f32)
    for k, column in enumerate(columns):
        out = jnp.where(lane == k, column, out)
    return out.astype(bf16)


def span(i, size, start=0):
    return pl.ds(pl.multiple_of(start + i * size, size), size)


def mm(a, b, ca, cb):
    return lax.dot_general(a, b, (((ca,), (cb,)), ((), ())), preferred_element_type=f32)


def place_of():
    w = lax.axis_index("wide")
    return w, w // 4, (w // 2) % 2, w % 2


def count_before(sel_col, ids):
    return jnp.sum(jnp.where(sel_col < ids, 1, 0).astype(i32), axis=0, keepdims=True)


def compact_of(i):
    n = lax.axis_index("narrow")
    r = (i * 1366) >> 16
    block = (r & 4 ^ n & 4) | ((r + n) & 3)
    return i + (block - r) * 48


def placement(sel_col, begin, size):
    _, z, y, c = place_of()
    slot = begin + lax.broadcasted_iota(i32, (1, size), 1)
    n = (slot * 2731) >> 16
    k = slot - n * CAP
    zz = (z + ((n >> 1) & 7) + 5) & 7
    block = zz * 4 + (y ^ (n & 1)) * 2 + (c ^ (n >> 4))
    start = count_before(sel_col, block * TOK)
    end = count_before(sel_col, block * TOK + TOK)
    row = compact_of(lax.broadcasted_iota(i32, (SEL, 1), 0))
    return jnp.where((row == start + k) & (row < end), 1.0, 0.0)


def pick_of(sel_row):
    w, _, _, _ = place_of()

    def before(ids):
        return jnp.sum(jnp.where(sel_row < ids, 1, 0).astype(i32), axis=1, keepdims=True)

    ids = w * TOK + lax.broadcasted_iota(i32, (TOK, 1), 0)
    first = before(jnp.full((1, 1), w * TOK, i32))
    last = before(jnp.full((1, 1), w * TOK + TOK, i32))
    rank = before(ids) - first
    marked = before(ids + 1) - before(ids) > 0
    k = lax.broadcasted_iota(i32, (TOK, CAP), 1)
    return jnp.where((k == rank) & marked, 1.0, 0.0).astype(bf16), first, last


def own_kernel(sel_hbm, tok_hbm, go_hbm, out, row, sel, tok, go, sems):
    copies = [
        pltpu.make_async_copy(tok_hbm, tok, sems.at[0]),
        pltpu.make_async_copy(go_hbm, go, sems.at[1]),
        pltpu.make_async_copy(sel_hbm, sel, sems.at[2]),
    ]
    for copy in copies:
        copy.start()
    copies[2].wait()
    sel_row = sel[...].reshape(1, SEL)
    row[...] = sel_row
    pick = pick_of(sel_row)[0]
    for n, held in enumerate((tok, go)):
        copies[n].wait()
        out[:, n * W : n * W + W] = mm(pick, held[...], 0, 0).astype(bf16)


def onehot_kernel(sel_row, *refs):
    sources, (put, spread, vectors), held, sems = refs[:2], refs[2:5], refs[5:7], refs[7]
    loads = [pltpu.make_async_copy(sources[n], held[n], sems.at[n]) for n in range(2)]
    for load in loads:
        load.start()
    eye = lax.broadcasted_iota(i32, (SEL, SEL), 0) == lax.broadcasted_iota(i32, (SEL, SEL), 1)
    sel_col = jnp.sum(jnp.where(eye, sel_row[...], 0), axis=1, keepdims=True)

    @pl.loop(0, 2 * SEL // 128)
    def _(i):
        hot = placement(sel_col, i * 128, 128)
        put[:, span(i, 128)] = hot.astype(bf16)
        spread[span(i, 128), :] = hot.T.astype(bf16)

    for load in loads:
        load.wait()
    vectors[0:1, :] = held[0][...]
    vectors[1:2, :] = held[1][...]


def stage_kernel(*refs):
    sources, piece, held, out, sems = refs[:3], refs[3], refs[5:8], refs[8], refs[9]
    loads = [pltpu.make_async_copy(sources[n], held[n], sems.at[n]) for n in range(3)]
    for load in loads:
        load.start()
    out[...] = piece[...]
    for load in loads:
        load.wait()


def forward_kernel(*refs):
    parts = refs[:16]
    put, vectors, *held, sel, gsel, keep = refs[16:24]
    to_up, to_down, to_y, near_up, near_down, slots, scaled = refs[24:]

    def write(lo, hi, value):
        value = value.astype(bf16)
        for r, (out, at) in enumerate(
            (
                (keep, 0),
                (near_up, 0),
                (keep, 96),
                (near_down, 0),
                (keep, 48),
                (to_up, 0),
                (to_y, 0),
                (to_down, 0),
            )
        ):
            out[at : at + 48, lo:hi] = value[48 * r : 48 * r + 48]

    for p in range(16):
        slots[48 * p : 48 * p + 48, :] = parts[p][...]
    squares = jnp.zeros((SEL, 128), f32)
    logit = jnp.zeros((SEL, 128), f32)
    for lo in range(0, W, WIDER):
        hi = lo + WIDER
        tile = mm(put[...], slots[:, lo:hi], 1, 0)
        sel[:, lo:hi] = tile.astype(bf16)
        for m in range(0, WIDER, 128):
            lanes = tile[:, m : m + 128]
            squares += lanes * lanes
            logit += lanes * vectors[1:2, lo + m : lo + m + 128]
        scaled[:, lo:hi] = (tile * (vectors[0:1, lo:hi] * DOWN)).astype(bf16)
    squares = jnp.sum(squares, axis=1, keepdims=True)
    logit = jnp.sum(logit, axis=1, keepdims=True)
    write(3 * W, ROW, lanes_of(heads(squares, 3) + heads(logit, 3), SEL))
    for n in range(2):
        for lo in range(0, W, WIDER):
            write(n * W + lo, n * W + lo + WIDER, mm(scaled[...], held[n][:, lo : lo + WIDER], 1, 0))
    for lo in range(W, 2 * W, WIDER):
        gsel[:, lo - W : lo - W + WIDER] = mm(put[...], slots[:, lo : lo + WIDER], 1, 0).astype(
            bf16
        )
    for lo in range(0, W, WIDER):
        write(2 * W + lo, 2 * W + lo + WIDER, mm(gsel[...], held[2][lo : lo + WIDER, :], 1, 1))


def stats(refs):
    tail = 0.0
    for ref in refs:
        tail = tail + ref[:, 3 * W :].astype(f32)
    return (
        tail[:, 0:1] + tail[:, 1:2] + tail[:, 2:3],
        tail[:, 3:4] + tail[:, 4:5] + tail[:, 5:6],
    )


def sum_kernel(keep, from_below, from_above, from_y, to_y, to_far):
    for out, refs in (
        (to_y, (keep.at[48:96], from_below, from_above)),
        (to_far, (keep.at[96:144], from_y)),
    ):

        @pl.loop(0, 3 * W // WIDER)
        def _(k, out=out, refs=refs):
            cols = span(k, WIDER)
            total = refs[0][:, cols].astype(f32)
            for ref in refs[1:]:
                total = total + ref[:, cols].astype(f32)
            out[:, cols] = total.astype(bf16)

        squares, logit = stats(refs)
        out[:, 3 * W :] = lanes_of(heads(squares, 3) + heads(logit, 3), SEL // 8)


def hidden_kernel(keep, near_below, near_above, from_y, from_far, out):
    rows = SEL // 8
    refs = (keep.at[0:48], near_below, near_above, from_y, from_far)

    squares, logit = stats(refs)
    scale = lax.rsqrt(squares / D + EPS)

    def tile(i, carry):
        router_grad, inner = carry

        def total(start):
            cols = span(i, WIDER, start)
            value = refs[0][:, cols].astype(f32)
            for ref in refs[1:]:
                value = value + ref[:, cols].astype(f32)
            return value

        gate = total(0) * (scale * UP)
        upv = total(W) * (scale * UP)
        back = total(2 * W)
        sigma = jax.nn.sigmoid(gate)
        hidden = (gate * sigma * upv).astype(bf16)
        d_hidden = logit * back
        d_gate = (d_hidden * upv * (sigma + gate * sigma * (1.0 - sigma))).astype(bf16)
        d_up = (d_hidden * gate * sigma).astype(bf16)
        router_grad += jnp.sum(hidden.astype(f32) * back, axis=1, keepdims=True)
        inner += jnp.sum(
            d_gate.astype(f32) * gate + d_up.astype(f32) * upv, axis=1, keepdims=True
        )
        out[:, span(i, WIDER)] = d_gate
        out[:, span(i, WIDER, W)] = d_up
        out[:, span(i, WIDER, 2 * W)] = hidden
        return router_grad, inner

    zero = jnp.zeros((rows, 1), f32)
    router_grad, inner = lax.fori_loop(0, W // WIDER, tile, (zero, zero))
    out[:, 3 * W :] = lanes_of(
        heads(scale, 3) + heads(logit, 3) + heads(router_grad, 3) + heads(inner, 3), rows
    )


def with_small(rows, small):
    return jnp.concatenate([rows] + heads(small, 2), axis=0).astype(bf16)


def apart(ref, cols):
    value = ref[:, cols].astype(f32)
    n = value.shape[0] - 8
    return value[:n], value[n : n + 4] + value[n + 4 : n + 8]


def to_row(column):
    eye = lax.broadcasted_iota(i32, (SEL, SEL), 0) == lax.broadcasted_iota(i32, (SEL, SEL), 1)
    return jnp.sum(jnp.where(eye, column, 0.0), axis=0, keepdims=True)


def normed_kernel(
    spread, own, above, b2, below, b4, b6, wg, wu, sel, theirs, ours, small, gd, cols
):
    j = pl.program_id(0)

    @pl.when(j == 0)
    def _():
        tail = []
        for r, (ref, at) in enumerate(
            (
                (own, 0),
                (above, 0),
                (b2, 0),
                (below, 0),
                (b4, 0),
                (above, 48),
                (b6, 0),
                (below, 48),
            )
        ):
            gd[48 * r : 48 * r + 48, :] = ref[at : at + 48, 0 : 2 * W]
            tail.append(ref[at : at + 48, 3 * W :].astype(f32))
        tail = jnp.concatenate(tail, axis=0)
        lane = lax.broadcasted_iota(i32, (SEL, 128), 1)

        def value(k):
            return jnp.sum(
                jnp.where((lane >= 3 * k) & (lane < 3 * k + 3), tail, 0.0), axis=1, keepdims=True
            )

        scale, router_grad, inner = value(0), value(2), value(3)
        cols[...] = jnp.where(lane == 0, scale, router_grad)
        small[...] = jnp.zeros(small.shape, f32)
        small[2:3, 0:SEL] = to_row(router_grad)
        small[2:3, SEL : 2 * SEL] = to_row(inner)
        small[3:4, 0:SEL] = to_row(scale)

    part = mm(gd[:, 0:W], wg[...], 1, 1) + mm(gd[:, W : 2 * W], wu[...], 1, 1)
    sel32 = sel[...].astype(f32)
    at = pl.ds(pl.multiple_of(j * W, W), W)
    small[0:1, at] = jnp.sum(part * sel32 * cols[:, 0:1], axis=0, keepdims=True)
    small[1:2, at] = jnp.sum(sel32 * cols[:, 1:2], axis=0, keepdims=True)
    rounded = part.astype(bf16)
    ours[...] = mm(spread[:SEL, :], rounded, 1, 0).astype(bf16)
    theirs[...] = with_small(mm(spread[SEL:, :], rounded, 1, 0), small[0:4, at])


def join_kernel(ours, theirs, mine, up3, down3, far, up1, down1, small):
    @pl.loop(0, W // TILE)
    def _(i):
        cols = span(i, TILE)
        rows, other = apart(theirs, cols)
        total = mine[0:4, cols] + other
        small[:, cols] = total
        for n, out in ((0, down3), (2, down1), (4, up1), (6, up3), (7, far)):
            at = slice(48 * n, 48 * n + 48)
            out[:, cols] = with_small(ours[at, cols].astype(f32) + rows[at], total)


def relay_kernel(
    up2, up2_other, from_below, down2, down2_other, from_above, far, small, to_up, to_down
):
    _, _, _, c = place_of()

    @pl.loop(0, W // TILE)
    def _(i):
        cols = span(i, TILE)
        rows, one = apart(far, cols)
        for base, other, ref, mask, out in (
            (up2, up2_other, from_below, c == 0, to_up),
            (down2, down2_other, from_above, c == 1, to_down),
        ):
            chunk, two = apart(ref, cols)
            chunk += base[:, cols].astype(f32) + other[:, cols].astype(f32)
            out[:, cols] = with_small(
                chunk + jnp.where(mask, rows, 0.0),
                small[:, cols] + two + jnp.where(mask, one, 0.0),
            )


def pair_kernel(stay, stay_other, small, a, b, c, d, here, there):
    @pl.loop(0, W // TILE)
    def _(i):
        cols = span(i, TILE)
        total = stay[:, cols].astype(f32) + stay_other[:, cols].astype(f32)
        low = small[:, cols]
        for part in (a, b, c, d):
            rows, other = apart(part, cols)
            total, low = total + rows, low + other
        here[0:CAP, cols] = total[:CAP]
        here[CAP : CAP + 4, cols] = low
        there[:, cols] = with_small(total[CAP:], low)


def far_kernel(below, above, _, out):
    out[...] = jnp.where(place_of()[3] == 0, below[...], above[...])


def final_kernel(
    here, there, mine, go, vectors, sel_row, small, grad_x, d_gain, d_router, held
):
    pick, first, last = pick_of(sel_row[...])
    own, summed = apart(there, slice(0, W))
    own = own + here[0:CAP, :]
    summed = summed + here[CAP : CAP + 4, :]
    d_gain[...] = summed[0:1]
    d_router[...] = summed[1:2]
    row = compact_of(lax.broadcasted_iota(i32, (1, SEL), 1))
    k = lax.broadcasted_iota(i32, (CAP, SEL), 0)
    where = (row == first + k) & (row < last)

    def place(values):
        return jnp.sum(jnp.where(where, values, 0.0), axis=1, keepdims=True)

    scale = place(small[3:4, 0:SEL])
    router_grad = place(summed[2:3, 0:SEL])
    inner = place(summed[2:3, SEL : 2 * SEL])
    held[...] = own

    @pl.loop(0, W // TILE)
    def _(i):
        cols = span(i, TILE)
        d_sel = (
            scale * vectors[0:1, cols] * held[:, cols]
            - mine[:, cols].astype(f32) * (scale * scale * inner / D)
            + router_grad * vectors[1:2, cols]
        )
        spread = jnp.zeros((TOK, TILE), f32)
        for piece in heads(d_sel, 3):
            spread += mm(pick, piece.astype(bf16), 1, 0)
        grad_x[:, cols] = (go[:, cols].astype(f32) + spread).astype(bf16)


def gather(pair, after, *weights):
    held = {0: pair}
    for k in (1, 2, 3):
        held[-k] = along(held[1 - k], 1)
        held[k] = along(held[k - 1], -1)
    far = pl.pallas_call(
        far_kernel,
        out_shape=jax.ShapeDtypeStruct(pair.shape, bf16),
        in_specs=[VMEM] * 2 + [pl.BlockSpec(memory_space=pl.ANY)],
        out_specs=VMEM,
        compiler_params=params(16),
        name="far",
    )(held[-2], held[2], after)
    held[4] = lax.ppermute(far, "wide", ZFAR)
    anywhere = pl.BlockSpec(memory_space=pl.ANY)
    *weights, above = pl.pallas_call(
        stage_kernel,
        out_shape=(jax.ShapeDtypeStruct((W, W), bf16),) * 3
        + (jax.ShapeDtypeStruct(pair.shape, bf16),),
        in_specs=[anywhere] * 3 + [VMEM, anywhere],
        out_specs=(VMEM,) * 4,
        scratch_shapes=[pltpu.SemaphoreType.DMA((3,))],
        compiler_params=params(16),
        name="stage",
    )(*weights, held[2], far)
    ours = [held[k] for k in range(-3, 5)]
    sent = ours[:5] + [above] + ours[6:]
    return ours + [lax.ppermute(piece, "wide", CORE) for piece in sent], weights


def local(tokens, grad_out, selected, gain, router_weight, w_gate, w_up, w_down):
    gain = gain.reshape(1, W)
    router_weight = router_weight.reshape(1, W)
    anywhere = pl.BlockSpec(memory_space=pl.ANY)
    mine, sel_row = pl.pallas_call(
        own_kernel,
        out_shape=(
            jax.ShapeDtypeStruct((CAP, 2 * W), bf16),
            jax.ShapeDtypeStruct((1, SEL), i32),
        ),
        in_specs=[anywhere] * 3,
        out_specs=(VMEM, VMEM),
        scratch_shapes=[pltpu.VMEM((SEL,), i32)]
        + [pltpu.VMEM((TOK, W), bf16)] * 2
        + [pltpu.SemaphoreType.DMA((3,))],
        compiler_params=params(60),
        name="own",
    )(selected, tokens, grad_out)
    put, spread, vectors = pl.pallas_call(
        onehot_kernel,
        out_shape=(
            jax.ShapeDtypeStruct((SEL, 2 * SEL), bf16),
            jax.ShapeDtypeStruct((2 * SEL, SEL), bf16),
            jax.ShapeDtypeStruct((2, W), f32),
        ),
        in_specs=[VMEM] + [anywhere] * 2,
        out_specs=(VMEM,) * 3,
        scratch_shapes=[pltpu.VMEM((1, W), f32)] * 2 + [pltpu.SemaphoreType.DMA((2,))],
        compiler_params=params(16),
        name="onehot",
    )(sel_row, gain, router_weight)
    pair = jnp.concatenate([mine, lax.ppermute(mine, "wide", YLO)], axis=0)
    parts, weights = gather(pair, put, w_gate, w_up, w_down)

    full = lambda *shape: pl.BlockSpec(shape, lambda j: (0,) * len(shape))
    block = jax.ShapeDtypeStruct((48, ROW), bf16)
    sel, gsel, keep, to_up, to_down, to_y, *near = pl.pallas_call(
        forward_kernel,
        out_shape=(
            jax.ShapeDtypeStruct((SEL, W), bf16),
            jax.ShapeDtypeStruct((SEL, W), bf16),
            jax.ShapeDtypeStruct((144, ROW), bf16),
        )
        + (block,) * 5,
        in_specs=[VMEM] * 21,
        out_specs=(VMEM,) * 8,
        scratch_shapes=[pltpu.VMEM((768, 2 * W), bf16), pltpu.VMEM((SEL, W), bf16)],
        compiler_params=params(16),
        cost_estimate=cost(3.6e9, 16e6),
        name="forward",
    )(*parts, put, vectors, *weights)

    from_below = lax.ppermute(to_up, "narrow", XUP)
    from_above = lax.ppermute(to_down, "narrow", XDOWN)
    from_y = lax.ppermute(to_y, "narrow", YHI)
    near = lax.ppermute(near[0], "narrow", XUP), lax.ppermute(near[1], "narrow", XDOWN)
    to_y, to_far = pl.pallas_call(
        sum_kernel,
        out_shape=(block, block),
        in_specs=[VMEM] * 4,
        out_specs=(VMEM, VMEM),
        compiler_params=params(8),
        name="sum",
    )(keep, from_below, from_above, from_y)
    from_far = lax.ppermute(to_far, "narrow", XFAR)
    from_y = lax.ppermute(to_y, "narrow", YHI)
    own = pl.pallas_call(
        hidden_kernel,
        out_shape=block,
        in_specs=[VMEM] * 5,
        out_specs=VMEM,
        compiler_params=params(8),
        name="hidden",
    )(keep, *near, from_y, from_far)

    b2 = lax.ppermute(own, "narrow", XFAR)
    b4 = lax.ppermute(own, "narrow", YHI)
    column = jnp.concatenate([own, b4], axis=0)
    below = lax.ppermute(column, "narrow", XUP)
    above = lax.ppermute(column, "narrow", XDOWN)
    b6 = lax.ppermute(b2, "narrow", YHI)

    theirs, ours, small = pl.pallas_call(
        normed_kernel,
        grid=(W // W,),
        out_shape=(
            jax.ShapeDtypeStruct((SEL + 8, W), bf16),
            jax.ShapeDtypeStruct((SEL, W), bf16),
            jax.ShapeDtypeStruct((8, W), f32),
        ),
        in_specs=[VMEM] * 7
        + [pl.BlockSpec((W, W), lambda j: (j, 0))] * 2
        + [pl.BlockSpec((SEL, W), lambda j: (0, j))],
        out_specs=(
            pl.BlockSpec((SEL + 8, W), lambda j: (0, j)),
            pl.BlockSpec((SEL, W), lambda j: (0, j)),
            full(8, W),
        ),
        scratch_shapes=[pltpu.VMEM((SEL, 2 * W), bf16), pltpu.VMEM((SEL, 128), f32)],
        compiler_params=params(),
        cost_estimate=cost(2.4e9, 9e6),
        name="normed",
    )(spread, own, above, b2, below, b4, b6, w_gate, w_up, sel)

    part = jax.ShapeDtypeStruct((56, W), bf16)
    theirs = lax.ppermute(theirs, "wide", CORE)
    up3, down3, far, up1, down1, total = pl.pallas_call(
        join_kernel,
        out_shape=(part,) * 5 + (jax.ShapeDtypeStruct((4, W), f32),),
        in_specs=[VMEM] * 3,
        out_specs=(VMEM,) * 6,
        compiler_params=params(16),
        name="join",
    )(ours, theirs, small)
    from_below, from_above = along(up3, 1), along(down3, -1)
    far = lax.ppermute(far, "wide", ZFAR)
    near = along(up1, 1), along(down1, -1)

    def chunk(n):
        return pl.BlockSpec((48, W), lambda j: (n, 0))

    up2, down2 = pl.pallas_call(
        relay_kernel,
        grid=(1,),
        out_shape=(part, part),
        in_specs=[chunk(5), chunk(5), full(56, W), chunk(1), chunk(1)]
        + [full(56, W), full(56, W), full(4, W)],
        out_specs=(full(56, W), full(56, W)),
        compiler_params=params(16),
        name="relay",
    )(ours, theirs, from_below, ours, theirs, from_above, far, total)
    here, there = pl.pallas_call(
        pair_kernel,
        grid=(1,),
        out_shape=(
            jax.ShapeDtypeStruct((CAP + 4, W), f32),
            jax.ShapeDtypeStruct((CAP + 8, W), bf16),
        ),
        in_specs=[chunk(3), chunk(3), full(4, W)] + [full(56, W)] * 4,
        out_specs=(full(CAP + 4, W), full(CAP + 8, W)),
        compiler_params=params(16),
        name="pair",
    )(ours, theirs, total, *near, along(up2, 2), along(down2, -2))
    there = lax.ppermute(there, "wide", YLO)

    rows = jnp.concatenate([own, above[:48], b2, below[:48], b4, above[48:], b6, below[48:]])
    tail = rows[:, 3 * W :].astype(f32)
    scale = jnp.sum(tail[:, 0:3], axis=1, keepdims=True)
    logit = jnp.sum(tail[:, 3:6], axis=1, keepdims=True)
    normed = (sel.astype(f32) * scale * gain).astype(bf16)
    d_out = (logit * gsel.astype(f32)).astype(bf16)
    grad_gate = mm(normed, rows[:, :W], 0, 0).astype(bf16)
    grad_up = mm(normed, rows[:, W : 2 * W], 0, 0).astype(bf16)
    grad_down = mm(rows[:, 2 * W : 3 * W], d_out, 0, 0).astype(bf16)

    vector = jax.ShapeDtypeStruct((1, W), f32)
    grad_x, d_gain, d_router = pl.pallas_call(
        final_kernel,
        out_shape=(jax.ShapeDtypeStruct((TOK, W), bf16), vector, vector),
        in_specs=[VMEM] * 7,
        out_specs=(VMEM,) * 3,
        scratch_shapes=[pltpu.VMEM((CAP, W), f32)],
        compiler_params=params(16),
        name="final",
    )(here, there, mine, grad_out, vectors, sel_row, small)
    return (grad_x, grad_gate, grad_up, grad_down, d_gain.reshape(W), d_router.reshape(W))


def solution(mesh):
    return jax.shard_map(
        local,
        mesh=mesh,
        in_specs=(
            P("wide", "narrow"),
            P("wide", "narrow"),
            P(),
            P("narrow"),
            P("narrow"),
            P("narrow", "wide"),
            P("narrow", "wide"),
            P("wide", "narrow"),
        ),
        out_specs=(
            P("wide", "narrow"),
            P("narrow", "wide"),
            P("narrow", "wide"),
            P("wide", "narrow"),
            P("narrow"),
            P("narrow"),
        ),
        check_vma=False,
    )
```

```python
import jax
import jax.numpy as jnp
from jax import lax
from jax.experimental import pallas as pl
from jax.experimental.pallas import tpu as pltpu
from jax.sharding import PartitionSpec as P

D = 8192
EPS = 1e-06
bf16 = jnp.bfloat16
f32 = jnp.float32
i32 = jnp.int32
DOWN, UP = 2.0**-20, 2.0**20
TOK = 96
CAP = 24
SEL = 384
W = 1024
TILE = 256
WIDER = 512

WIDE = [(z, y, c) for z in range(8) for y in range(2) for c in range(2)]


def wide_pairs(move):
    def index(z, y, c):
        return (z % 8 * 2 + y) * 2 + c

    return [(index(*t), index(*move(*t))) for t in WIDE]


CORE = wide_pairs(lambda z, y, c: (z, y, 1 - c))
YLO = wide_pairs(lambda z, y, c: (z, 1 - y, c))
XUP = [(n, n // 4 * 4 + (n + 1) % 4) for n in range(8)]
XDOWN = [(n, n // 4 * 4 + (n + 3) % 4) for n in range(8)]
XFAR = [(n, n // 4 * 4 + (n + 2) % 4) for n in range(8)]
YHI = [(n, (n + 4) % 8) for n in range(8)]
ROW = 3 * 1024 + 128
ZFAR = wide_pairs(lambda z, y, c: (z + 2 + 4 * c, y, c))


def along(value, step):
    return lax.ppermute(value, "wide", wide_pairs(lambda z, y, c: (z + 8 + step, y, c)))


VMEM = pl.BlockSpec(memory_space=pltpu.VMEM)


def params(mib=24):
    return pltpu.CompilerParams(vmem_limit_bytes=mib << 20)


def cost(flops, bytes_):
    return pl.CostEstimate(flops=int(flops), bytes_accessed=int(bytes_), transcendentals=0)


def heads(value, count):
    out = []
    for _ in range(count):
        head = value.astype(bf16).astype(f32)
        out.append(head)
        value = jnp.where(jnp.abs(head) < jnp.inf, value - head, 0.0)
    return out


def lanes_of(columns, rows):
    lane = lax.broadcasted_iota(i32, (rows, 128), 1)
    out = jnp.zeros((rows, 128), f32)
    for k, column in enumerate(columns):
        out = jnp.where(lane == k, column, out)
    return out.astype(bf16)


def span(i, size, start=0):
    return pl.ds(pl.multiple_of(start + i * size, size), size)


def mm(a, b, ca, cb):
    return lax.dot_general(a, b, (((ca,), (cb,)), ((), ())), preferred_element_type=f32)


def place_of():
    w = lax.axis_index("wide")
    return w, w // 4, (w // 2) % 2, w % 2


def count_before(sel_col, ids):
    return jnp.sum(jnp.where(sel_col < ids, 1, 0).astype(i32), axis=0, keepdims=True)


def compact_of(i):
    n = lax.axis_index("narrow")
    r = (i * 1366) >> 16
    block = (r & 4 ^ n & 4) | ((r + n) & 3)
    return i + (block - r) * 48


def placement(sel_col, begin, size):
    _, z, y, c = place_of()
    slot = begin + lax.broadcasted_iota(i32, (1, size), 1)
    n = (slot * 2731) >> 16
    k = slot - n * CAP
    zz = (z + ((n >> 1) & 7) + 5) & 7
    block = zz * 4 + (y ^ (n & 1)) * 2 + (c ^ (n >> 4))
    start = count_before(sel_col, block * TOK)
    end = count_before(sel_col, block * TOK + TOK)
    row = compact_of(lax.broadcasted_iota(i32, (SEL, 1), 0))
    return jnp.where((row == start + k) & (row < end), 1.0, 0.0)


def pick_of(sel_row):
    w, _, _, _ = place_of()

    def before(ids):
        return jnp.sum(jnp.where(sel_row < ids, 1, 0).astype(i32), axis=1, keepdims=True)

    ids = w * TOK + lax.broadcasted_iota(i32, (TOK, 1), 0)
    first = before(jnp.full((1, 1), w * TOK, i32))
    last = before(jnp.full((1, 1), w * TOK + TOK, i32))
    rank = before(ids) - first
    marked = before(ids + 1) - before(ids) > 0
    k = lax.broadcasted_iota(i32, (TOK, CAP), 1)
    return jnp.where((k == rank) & marked, 1.0, 0.0).astype(bf16), first, last


def own_kernel(sel_hbm, tok_hbm, go_hbm, gain_hbm, rw_hbm, out, row, vectors, *held):
    *held, sems = held
    sources = (sel_hbm, tok_hbm, go_hbm, gain_hbm, rw_hbm)
    copies = [pltpu.make_async_copy(sources[n], held[n], sems.at[n]) for n in range(5)]
    for copy in copies:
        copy.start()
    copies[0].wait()
    sel_row = held[0][...].reshape(1, SEL)
    row[...] = sel_row
    pick = pick_of(sel_row)[0]
    for n in range(2):
        copies[1 + n].wait()
        out[:, n * W : n * W + W] = mm(pick, held[1 + n][...], 0, 0).astype(bf16)
    for n in range(2):
        copies[3 + n].wait()
        vectors[n : n + 1, :] = held[3 + n][...]


def onehot_kernel(sel_row, put, spread):
    eye = lax.broadcasted_iota(i32, (SEL, SEL), 0) == lax.broadcasted_iota(i32, (SEL, SEL), 1)
    sel_col = jnp.sum(jnp.where(eye, sel_row[...], 0), axis=1, keepdims=True)

    @pl.loop(0, 2 * SEL // 128)
    def _(i):
        hot = placement(sel_col, i * 128, 128)
        put[:, span(i, 128)] = hot.astype(bf16)
        spread[span(i, 128), :] = hot.T.astype(bf16)


def stage_kernel(*refs):
    sources, piece, held, out, sems = refs[:3], refs[3], refs[5:8], refs[8], refs[9]
    loads = [pltpu.make_async_copy(sources[n], held[n], sems.at[n]) for n in range(3)]
    for load in loads:
        load.start()
    out[...] = piece[...]
    for load in loads:
        load.wait()


def forward_kernel(*refs):
    parts = refs[:16]
    put, vectors, *held, sel, gsel, keep = refs[16:24]
    to_up, to_down, to_y, near_up, near_down, slots, scaled = refs[24:]

    def write(lo, hi, value):
        value = value.astype(bf16)
        for r, (out, at) in enumerate(
            (
                (keep, 0),
                (near_up, 0),
                (keep, 96),
                (near_down, 0),
                (keep, 48),
                (to_up, 0),
                (to_y, 0),
                (to_down, 0),
            )
        ):
            out[at : at + 48, lo:hi] = value[48 * r : 48 * r + 48]

    for p in range(16):
        slots[48 * p : 48 * p + 48, :] = parts[p][...]
    squares = jnp.zeros((SEL, 128), f32)
    logit = jnp.zeros((SEL, 128), f32)
    for lo in range(0, W, WIDER):
        hi = lo + WIDER
        tile = mm(put[...], slots[:, lo:hi], 1, 0)
        sel[:, lo:hi] = tile.astype(bf16)
        for m in range(0, WIDER, 128):
            lanes = tile[:, m : m + 128]
            squares += lanes * lanes
            logit += lanes * vectors[1:2, lo + m : lo + m + 128]
        scaled[:, lo:hi] = (tile * (vectors[0:1, lo:hi] * DOWN)).astype(bf16)
    squares = jnp.sum(squares, axis=1, keepdims=True)
    logit = jnp.sum(logit, axis=1, keepdims=True)
    write(3 * W, ROW, lanes_of(heads(squares, 3) + heads(logit, 3), SEL))
    for n in range(2):
        for lo in range(0, W, WIDER):
            write(n * W + lo, n * W + lo + WIDER, mm(scaled[...], held[n][:, lo : lo + WIDER], 1, 0))
    for lo in range(W, 2 * W, WIDER):
        gsel[:, lo - W : lo - W + WIDER] = mm(put[...], slots[:, lo : lo + WIDER], 1, 0).astype(
            bf16
        )
    for lo in range(0, W, WIDER):
        write(2 * W + lo, 2 * W + lo + WIDER, mm(gsel[...], held[2][lo : lo + WIDER, :], 1, 1))


def stats(refs):
    tail = 0.0
    for ref in refs:
        tail = tail + ref[:, 3 * W :].astype(f32)
    return (
        tail[:, 0:1] + tail[:, 1:2] + tail[:, 2:3],
        tail[:, 3:4] + tail[:, 4:5] + tail[:, 5:6],
    )


def sum_kernel(keep, from_below, from_above, from_y, to_y, to_far):
    for out, refs in (
        (to_y, (keep.at[48:96], from_below, from_above)),
        (to_far, (keep.at[96:144], from_y)),
    ):

        @pl.loop(0, 3 * W // W)
        def _(k, out=out, refs=refs):
            cols = span(k, W)
            total = refs[0][:, cols].astype(f32)
            for ref in refs[1:]:
                total = total + ref[:, cols].astype(f32)
            out[:, cols] = total.astype(bf16)

        squares, logit = stats(refs)
        out[:, 3 * W :] = lanes_of(heads(squares, 3) + heads(logit, 3), SEL // 8)


def hidden_kernel(keep, near_below, near_above, from_y, from_far, out):
    rows = SEL // 8
    refs = (keep.at[0:48], near_below, near_above, from_y, from_far)

    squares, logit = stats(refs)
    scale = lax.rsqrt(squares / D + EPS)

    def tile(i, carry):
        router_grad, inner = carry

        def total(start):
            cols = span(i, WIDER, start)
            value = refs[0][:, cols].astype(f32)
            for ref in refs[1:]:
                value = value + ref[:, cols].astype(f32)
            return value

        gate = total(0) * (scale * UP)
        upv = total(W) * (scale * UP)
        back = total(2 * W)
        sigma = jax.nn.sigmoid(gate)
        hidden = (gate * sigma * upv).astype(bf16)
        d_hidden = logit * back
        d_gate = (d_hidden * upv * (sigma + gate * sigma * (1.0 - sigma))).astype(bf16)
        d_up = (d_hidden * gate * sigma).astype(bf16)
        router_grad += jnp.sum(hidden.astype(f32) * back, axis=1, keepdims=True)
        inner += jnp.sum(
            d_gate.astype(f32) * gate + d_up.astype(f32) * upv, axis=1, keepdims=True
        )
        out[:, span(i, WIDER)] = d_gate
        out[:, span(i, WIDER, W)] = d_up
        out[:, span(i, WIDER, 2 * W)] = hidden
        return router_grad, inner

    zero = jnp.zeros((rows, 1), f32)
    router_grad, inner = lax.fori_loop(0, W // WIDER, tile, (zero, zero))
    out[:, 3 * W :] = lanes_of(
        heads(scale, 3) + heads(logit, 3) + heads(router_grad, 3) + heads(inner, 3), rows
    )


def with_small(rows, small):
    return jnp.concatenate([rows] + heads(small, 2), axis=0).astype(bf16)


def apart(ref, cols):
    value = ref[:, cols].astype(f32)
    n = value.shape[0] - 8
    return value[:n], value[n : n + 4] + value[n + 4 : n + 8]


def to_row(column):
    eye = lax.broadcasted_iota(i32, (SEL, SEL), 0) == lax.broadcasted_iota(i32, (SEL, SEL), 1)
    return jnp.sum(jnp.where(eye, column, 0.0), axis=0, keepdims=True)


def normed_kernel(
    spread, own, above, b2, below, b4, b6, wg, wu, sel, theirs, ours, small, gd, cols
):
    j = pl.program_id(0)

    @pl.when(j == 0)
    def _():
        tail = []
        for r, (ref, at) in enumerate(
            (
                (own, 0),
                (above, 0),
                (b2, 0),
                (below, 0),
                (b4, 0),
                (above, 48),
                (b6, 0),
                (below, 48),
            )
        ):
            gd[48 * r : 48 * r + 48, :] = ref[at : at + 48, 0 : 2 * W]
            tail.append(ref[at : at + 48, 3 * W :].astype(f32))
        tail = jnp.concatenate(tail, axis=0)
        lane = lax.broadcasted_iota(i32, (SEL, 128), 1)

        def value(k):
            return jnp.sum(
                jnp.where((lane >= 3 * k) & (lane < 3 * k + 3), tail, 0.0), axis=1, keepdims=True
            )

        scale, router_grad, inner = value(0), value(2), value(3)
        cols[...] = jnp.where(lane == 0, scale, router_grad)
        small[...] = jnp.zeros(small.shape, f32)
        small[2:3, 0:SEL] = to_row(router_grad)
        small[2:3, SEL : 2 * SEL] = to_row(inner)
        small[3:4, 0:SEL] = to_row(scale)

    part = mm(gd[:, 0:W], wg[...], 1, 1) + mm(gd[:, W : 2 * W], wu[...], 1, 1)
    sel32 = sel[...].astype(f32)
    at = pl.ds(pl.multiple_of(j * W, W), W)
    small[0:1, at] = jnp.sum(part * sel32 * cols[:, 0:1], axis=0, keepdims=True)
    small[1:2, at] = jnp.sum(sel32 * cols[:, 1:2], axis=0, keepdims=True)
    rounded = part.astype(bf16)
    ours[...] = mm(spread[:SEL, :], rounded, 1, 0).astype(bf16)
    theirs[...] = with_small(mm(spread[SEL:, :], rounded, 1, 0), small[0:4, at])


def join_kernel(ours, theirs, mine, up3, down3, far, up1, down1, small):
    @pl.loop(0, W // TILE)
    def _(i):
        cols = span(i, TILE)
        rows, other = apart(theirs, cols)
        total = mine[0:4, cols] + other
        small[:, cols] = total
        for n, out in ((0, down3), (2, down1), (4, up1), (6, up3), (7, far)):
            at = slice(48 * n, 48 * n + 48)
            out[:, cols] = with_small(ours[at, cols].astype(f32) + rows[at], total)


def relay_kernel(
    up2, up2_other, from_below, down2, down2_other, from_above, far, small, to_up, to_down
):
    _, _, _, c = place_of()

    @pl.loop(0, W // TILE)
    def _(i):
        cols = span(i, TILE)
        rows, one = apart(far, cols)
        for base, other, ref, mask, out in (
            (up2, up2_other, from_below, c == 0, to_up),
            (down2, down2_other, from_above, c == 1, to_down),
        ):
            chunk, two = apart(ref, cols)
            chunk += base[:, cols].astype(f32) + other[:, cols].astype(f32)
            out[:, cols] = with_small(
                chunk + jnp.where(mask, rows, 0.0),
                small[:, cols] + two + jnp.where(mask, one, 0.0),
            )


def pair_kernel(stay, stay_other, small, a, b, c, d, here, there):
    @pl.loop(0, W // TILE)
    def _(i):
        cols = span(i, TILE)
        total = stay[:, cols].astype(f32) + stay_other[:, cols].astype(f32)
        low = small[:, cols]
        for part in (a, b, c, d):
            rows, other = apart(part, cols)
            total, low = total + rows, low + other
        here[0:CAP, cols] = total[:CAP]
        here[CAP : CAP + 4, cols] = low
        there[:, cols] = with_small(total[CAP:], low)


def far_kernel(below, above, _, out):
    out[...] = jnp.where(place_of()[3] == 0, below[...], above[...])


def final_kernel(
    here, there, mine, go, vectors, sel_row, small, grad_x, d_gain, d_router, held
):
    pick, first, last = pick_of(sel_row[...])
    own, summed = apart(there, slice(0, W))
    own = own + here[0:CAP, :]
    summed = summed + here[CAP : CAP + 4, :]
    d_gain[...] = summed[0:1]
    d_router[...] = summed[1:2]
    row = compact_of(lax.broadcasted_iota(i32, (1, SEL), 1))
    k = lax.broadcasted_iota(i32, (CAP, SEL), 0)
    where = (row == first + k) & (row < last)

    def place(values):
        return jnp.sum(jnp.where(where, values, 0.0), axis=1, keepdims=True)

    scale = place(small[3:4, 0:SEL])
    router_grad = place(summed[2:3, 0:SEL])
    inner = place(summed[2:3, SEL : 2 * SEL])
    held[...] = own

    @pl.loop(0, W // WIDER)
    def _(i):
        cols = span(i, WIDER)
        d_sel = (
            scale * vectors[0:1, cols] * held[:, cols]
            - mine[:, cols].astype(f32) * (scale * scale * inner / D)
            + router_grad * vectors[1:2, cols]
        )
        spread = jnp.zeros((TOK, WIDER), f32)
        for piece in heads(d_sel, 3):
            spread += mm(pick, piece.astype(bf16), 1, 0)
        grad_x[:, cols] = (go[:, cols].astype(f32) + spread).astype(bf16)


def gather(pair, after, *weights):
    held = {0: pair}
    for k in (1, 2, 3):
        held[-k] = along(held[1 - k], 1)
        held[k] = along(held[k - 1], -1)
    far = pl.pallas_call(
        far_kernel,
        out_shape=jax.ShapeDtypeStruct(pair.shape, bf16),
        in_specs=[VMEM] * 2 + [pl.BlockSpec(memory_space=pl.ANY)],
        out_specs=VMEM,
        compiler_params=params(16),
        name="far",
    )(held[-2], held[2], after)
    held[4] = lax.ppermute(far, "wide", ZFAR)
    anywhere = pl.BlockSpec(memory_space=pl.ANY)
    *weights, above = pl.pallas_call(
        stage_kernel,
        out_shape=(jax.ShapeDtypeStruct((W, W), bf16),) * 3
        + (jax.ShapeDtypeStruct(pair.shape, bf16),),
        in_specs=[anywhere] * 3 + [VMEM, anywhere],
        out_specs=(VMEM,) * 4,
        scratch_shapes=[pltpu.SemaphoreType.DMA((3,))],
        compiler_params=params(16),
        name="stage",
    )(*weights, held[2], far)
    ours = [held[k] for k in range(-3, 5)]
    sent = ours[:5] + [above] + ours[6:]
    return ours + [lax.ppermute(piece, "wide", CORE) for piece in sent], weights


def local(tokens, grad_out, selected, gain, router_weight, w_gate, w_up, w_down):
    gain = gain.reshape(1, W)
    router_weight = router_weight.reshape(1, W)
    anywhere = pl.BlockSpec(memory_space=pl.ANY)
    mine, sel_row, vectors = pl.pallas_call(
        own_kernel,
        out_shape=(
            jax.ShapeDtypeStruct((CAP, 2 * W), bf16),
            jax.ShapeDtypeStruct((1, SEL), i32),
            jax.ShapeDtypeStruct((2, W), f32),
        ),
        in_specs=[anywhere] * 5,
        out_specs=(VMEM,) * 3,
        scratch_shapes=[pltpu.VMEM((SEL,), i32)]
        + [pltpu.VMEM((TOK, W), bf16)] * 2
        + [pltpu.VMEM((1, W), f32)] * 2
        + [pltpu.SemaphoreType.DMA((5,))],
        compiler_params=params(60),
        name="own",
    )(selected, tokens, grad_out, gain, router_weight)
    put, spread = pl.pallas_call(
        onehot_kernel,
        out_shape=(
            jax.ShapeDtypeStruct((SEL, 2 * SEL), bf16),
            jax.ShapeDtypeStruct((2 * SEL, SEL), bf16),
        ),
        in_specs=[VMEM],
        out_specs=(VMEM,) * 2,
        compiler_params=params(16),
        name="onehot",
    )(sel_row)
    pair = jnp.concatenate([mine, lax.ppermute(mine, "wide", YLO)], axis=0)
    parts, weights = gather(pair, put, w_gate, w_up, w_down)

    full = lambda *shape: pl.BlockSpec(shape, lambda j: (0,) * len(shape))
    block = jax.ShapeDtypeStruct((48, ROW), bf16)
    sel, gsel, keep, to_up, to_down, to_y, *near = pl.pallas_call(
        forward_kernel,
        out_shape=(
            jax.ShapeDtypeStruct((SEL, W), bf16),
            jax.ShapeDtypeStruct((SEL, W), bf16),
            jax.ShapeDtypeStruct((144, ROW), bf16),
        )
        + (block,) * 5,
        in_specs=[VMEM] * 21,
        out_specs=(VMEM,) * 8,
        scratch_shapes=[pltpu.VMEM((768, 2 * W), bf16), pltpu.VMEM((SEL, W), bf16)],
        compiler_params=params(16),
        cost_estimate=cost(3.6e9, 16e6),
        name="forward",
    )(*parts, put, vectors, *weights)

    from_below = lax.ppermute(to_up, "narrow", XUP)
    from_above = lax.ppermute(to_down, "narrow", XDOWN)
    from_y = lax.ppermute(to_y, "narrow", YHI)
    near = lax.ppermute(near[0], "narrow", XUP), lax.ppermute(near[1], "narrow", XDOWN)
    to_y, to_far = pl.pallas_call(
        sum_kernel,
        out_shape=(block, block),
        in_specs=[VMEM] * 4,
        out_specs=(VMEM, VMEM),
        compiler_params=params(8),
        name="sum",
    )(keep, from_below, from_above, from_y)
    from_far = lax.ppermute(to_far, "narrow", XFAR)
    from_y = lax.ppermute(to_y, "narrow", YHI)
    own = pl.pallas_call(
        hidden_kernel,
        out_shape=block,
        in_specs=[VMEM] * 5,
        out_specs=VMEM,
        compiler_params=params(8),
        name="hidden",
    )(keep, *near, from_y, from_far)

    b2 = lax.ppermute(own, "narrow", XFAR)
    b4 = lax.ppermute(own, "narrow", YHI)
    column = jnp.concatenate([own, b4], axis=0)
    below = lax.ppermute(column, "narrow", XUP)
    above = lax.ppermute(column, "narrow", XDOWN)
    b6 = lax.ppermute(b2, "narrow", YHI)

    theirs, ours, small = pl.pallas_call(
        normed_kernel,
        grid=(W // W,),
        out_shape=(
            jax.ShapeDtypeStruct((SEL + 8, W), bf16),
            jax.ShapeDtypeStruct((SEL, W), bf16),
            jax.ShapeDtypeStruct((8, W), f32),
        ),
        in_specs=[VMEM] * 7
        + [pl.BlockSpec((W, W), lambda j: (j, 0))] * 2
        + [pl.BlockSpec((SEL, W), lambda j: (0, j))],
        out_specs=(
            pl.BlockSpec((SEL + 8, W), lambda j: (0, j)),
            pl.BlockSpec((SEL, W), lambda j: (0, j)),
            full(8, W),
        ),
        scratch_shapes=[pltpu.VMEM((SEL, 2 * W), bf16), pltpu.VMEM((SEL, 128), f32)],
        compiler_params=params(),
        cost_estimate=cost(2.4e9, 9e6),
        name="normed",
    )(spread, own, above, b2, below, b4, b6, w_gate, w_up, sel)

    part = jax.ShapeDtypeStruct((56, W), bf16)
    theirs = lax.ppermute(theirs, "wide", CORE)
    up3, down3, far, up1, down1, total = pl.pallas_call(
        join_kernel,
        out_shape=(part,) * 5 + (jax.ShapeDtypeStruct((4, W), f32),),
        in_specs=[VMEM] * 3,
        out_specs=(VMEM,) * 6,
        compiler_params=params(16),
        name="join",
    )(ours, theirs, small)
    from_below, from_above = along(up3, 1), along(down3, -1)
    far = lax.ppermute(far, "wide", ZFAR)
    near = along(up1, 1), along(down1, -1)

    def chunk(n):
        return pl.BlockSpec((48, W), lambda j: (n, 0))

    up2, down2 = pl.pallas_call(
        relay_kernel,
        grid=(1,),
        out_shape=(part, part),
        in_specs=[chunk(5), chunk(5), full(56, W), chunk(1), chunk(1)]
        + [full(56, W), full(56, W), full(4, W)],
        out_specs=(full(56, W), full(56, W)),
        compiler_params=params(16),
        name="relay",
    )(ours, theirs, from_below, ours, theirs, from_above, far, total)
    here, there = pl.pallas_call(
        pair_kernel,
        grid=(1,),
        out_shape=(
            jax.ShapeDtypeStruct((CAP + 4, W), f32),
            jax.ShapeDtypeStruct((CAP + 8, W), bf16),
        ),
        in_specs=[chunk(3), chunk(3), full(4, W)] + [full(56, W)] * 4,
        out_specs=(full(CAP + 4, W), full(CAP + 8, W)),
        compiler_params=params(16),
        name="pair",
    )(ours, theirs, total, *near, along(up2, 2), along(down2, -2))
    there = lax.ppermute(there, "wide", YLO)

    rows = jnp.concatenate([own, above[:48], b2, below[:48], b4, above[48:], b6, below[48:]])
    tail = rows[:, 3 * W :].astype(f32)
    scale = jnp.sum(tail[:, 0:3], axis=1, keepdims=True)
    logit = jnp.sum(tail[:, 3:6], axis=1, keepdims=True)
    normed = (sel.astype(f32) * scale * gain).astype(bf16)
    d_out = (logit * gsel.astype(f32)).astype(bf16)
    grad_gate = mm(normed, rows[:, :W], 0, 0).astype(bf16)
    grad_up = mm(normed, rows[:, W : 2 * W], 0, 0).astype(bf16)
    grad_down = mm(rows[:, 2 * W : 3 * W], d_out, 0, 0).astype(bf16)

    vector = jax.ShapeDtypeStruct((1, W), f32)
    grad_x, d_gain, d_router = pl.pallas_call(
        final_kernel,
        out_shape=(jax.ShapeDtypeStruct((TOK, W), bf16), vector, vector),
        in_specs=[VMEM] * 7,
        out_specs=(VMEM,) * 3,
        scratch_shapes=[pltpu.VMEM((CAP, W), f32)],
        compiler_params=params(16),
        name="final",
    )(here, there, mine, grad_out, vectors, sel_row, small)
    return (grad_x, grad_gate, grad_up, grad_down, d_gain.reshape(W), d_router.reshape(W))


def solution(mesh):
    return jax.shard_map(
        local,
        mesh=mesh,
        in_specs=(
            P("wide", "narrow"),
            P("wide", "narrow"),
            P(),
            P("narrow"),
            P("narrow"),
            P("narrow", "wide"),
            P("narrow", "wide"),
            P("wide", "narrow"),
        ),
        out_specs=(
            P("wide", "narrow"),
            P("narrow", "wide"),
            P("narrow", "wide"),
            P("wide", "narrow"),
            P("narrow"),
            P("narrow"),
        ),
        check_vma=False,
    )
```
